256 devices in a mesh: band: 16 (over x, y_hi, core), strip: 16 (over y_lo, z).
Axes of the slice: x: 4, y: 4 (y_hi: 2, y_lo: 2; y = y_hi * 2 + y_lo), z: 8, core: 2. Of those that a mesh axis runs over, the one named last changes fastest.
Arguments:
- pattern: int32 [131072, 2048], P(('band', 'strip')), may hold values from 0 to 2, as said below
Outputs:
- dose: float32 [131072, 2048], P(('band', 'strip'))
- exposure: float32 [131072, 2048], P(('band', 'strip'))
The draws below stay inside these ranges and needn't reach their ends.
Inputs may be any that keep to these rules, and one draw needn't show every extreme that they name: `pattern`: class codes: 0 clear, 1 feature interior, 2 feature edge.
All inputs are finite; a program needn't handle non-finite values.
Results may differ from the reference program's by a relative error of at most 0.0003.
Values sent between devices are 32-bit elements; how exact they have to be, the bound alone decides.
No kernel may reach another device: no remote copies, remote signals or barrier semaphores. Data moves between devices by JAX's collectives and lax.ppermute only.
A program may use at most 64 MiB of HBM per device.

```python
import math
import jax
import jax.numpy as jnp
from jax import lax

W = 2048
R = 512
POOL = 256
H = 16
ITERS = 2
NR = 131072
NRC = 512
NCC = 8


def draw_pattern(key, part):
    tile = max(1, POOL // 8)
    key_level, key_roll, key_kind, key_cap = jax.random.split(jax.random.fold_in(key, 11), 4)
    order = jax.random.permutation(key_cap, 8)
    caps = jnp.where(order < 4, 1, 5).astype(jnp.int32)
    tile_rows = NR // tile
    segment = (jnp.arange(tile_rows).astype(jnp.int32) * tile * 8 // NR).astype(jnp.int32)
    row_cap = caps[segment][:, None]
    raw = jax.random.randint(key_level, (tile_rows, W // tile), 0, 60)
    level = (raw % (row_cap + 1)).astype(jnp.int32)
    level = jnp.repeat(jnp.repeat(level, tile, axis=0), tile, axis=1)
    roll = jax.random.randint(key_roll, (NR, W), 0, 4)
    kind = jax.random.randint(key_kind, (NR, W), 1, 3)
    return jnp.where(roll < level, kind, 0).astype(jnp.int32)


def setup_inputs(seed: int = 0) -> dict:
    seeds = jax.random.split(jax.random.key(seed), 2)
    pattern = draw_pattern(jax.random.fold_in(seeds[1], 71), 0)
    return dict(pattern=pattern)


ETA_BACK = 0.75
SIGMA_BACK = 6.0

def fine_weight(diff):
    spread = H / 3.0
    steps = jnp.arange(-H, H + 1).astype(jnp.float32)
    total = jnp.sum(jnp.exp(-steps * steps / (2.0 * spread * spread)))
    inside = jnp.abs(diff) <= H
    return jnp.where(inside, jnp.exp(-diff * diff / (2.0 * spread * spread)) / total, 0.0).astype(jnp.float32)

def back_weight(diff, fog_sigma):
    near = jnp.exp(-diff * diff / (2.0 * SIGMA_BACK * SIGMA_BACK)) / (SIGMA_BACK * math.sqrt(2.0 * math.pi))
    far = jnp.exp(-diff * diff / (2.0 * fog_sigma * fog_sigma)) / (fog_sigma * math.sqrt(2.0 * math.pi))
    return (0.5 * near + 0.5 * far).astype(jnp.float32)

def reference(pattern):
    dose = jnp.where(pattern == 1, 1.0, jnp.where(pattern == 2, 1.4, 0.0)).astype(jnp.float32)
    taps = fine_weight(jnp.arange(-H, H + 1).astype(jnp.float32))
    fog_sigma = NRC / 4.0
    coarse_idx = jnp.arange(NRC).astype(jnp.float32)
    kernel_rows = back_weight(coarse_idx[None, :] - coarse_idx[:, None], fog_sigma)
    col_idx = jnp.arange(NCC).astype(jnp.float32)
    kernel_cols = back_weight(col_idx[:, None] - col_idx[None, :], fog_sigma)
    block_count = NR // R

    def iterate(step, carry):
        dose_now, previous = carry
        coarse = dose_now.reshape(NRC, POOL, NCC, POOL).sum(axis=(1, 3)) / (POOL * POOL)
        back = jnp.dot(kernel_rows, coarse, precision=lax.Precision.HIGHEST, preferred_element_type=jnp.float32)
        back = jnp.dot(back, kernel_cols, precision=lax.Precision.HIGHEST, preferred_element_type=jnp.float32)
        back_rows = jnp.repeat(back, POOL, axis=0)
        padded = jnp.pad(dose_now, ((H, H), (0, 0)))

        def one_block(index):
            start = (index * R).astype(jnp.int32)
            window = lax.dynamic_slice_in_dim(padded, start, R + 2 * H, 0)
            rows_blur = jnp.zeros((R, W), window.dtype)
            for shift in range(2 * H + 1):
                rows_blur = rows_blur + taps[shift] * window[shift:shift + R]
            padded_cols = jnp.pad(rows_blur, ((0, 0), (H, H)))
            forward = jnp.zeros_like(rows_blur)
            for shift in range(2 * H + 1):
                forward = forward + taps[shift] * padded_cols[:, shift:shift + W]
            local_back = lax.dynamic_slice_in_dim(back_rows, start, R, 0)
            upsampled = jnp.repeat(local_back, POOL, axis=1)
            exposure = (forward + ETA_BACK * upsampled) / (1.0 + ETA_BACK)
            local_pattern = lax.dynamic_slice_in_dim(pattern, start, R, 0)
            occupancy = (local_pattern > 0).astype(jnp.float32)
            target = jnp.where(local_pattern == 1, 0.5, jnp.where(local_pattern == 2, 0.55, 0.0)).astype(jnp.float32)
            local_dose = lax.dynamic_slice_in_dim(dose_now, start, R, 0)
            new_dose = occupancy * (local_dose + target - exposure)
            return (new_dose, exposure)
        new_blocks, exposure_blocks = lax.map(one_block, jnp.arange(block_count).astype(jnp.int32))
        return (new_blocks.reshape(NR, W), exposure_blocks.reshape(NR, W))
    dose, exposure = lax.fori_loop(0, ITERS, iterate, (dose, jnp.zeros_like(dose)))
    return (dose, exposure)
```

```python
import functools
import math

import jax
import jax.numpy as jnp
import ml_dtypes
import numpy as np
from jax import lax
from jax.experimental import pallas as pl
from jax.experimental.pallas import tpu as pltpu
from jax.sharding import PartitionSpec as P

POOL = 256
H = 16
ETA_BACK = 0.75
SIGMA_BACK = 6.0
TOTAL = 1.0 + ETA_BACK
BACK_SHARE = ETA_BACK / TOTAL
AXES = ("band", "strip")
F32 = jnp.float32
BF16 = jnp.bfloat16
LANES = 128


def fine_taps(diff):
    spread = H / 3.0
    steps = np.arange(-H, H + 1, dtype=np.float64)
    total = np.exp(-steps * steps / (2.0 * spread * spread)).sum()
    weight = np.exp(-diff * diff / (2.0 * spread * spread)) / total
    return np.where(np.abs(diff) <= H, weight, 0.0)


def back_weight(diff, fog_sigma):
    near = np.exp(-diff * diff / (2.0 * SIGMA_BACK * SIGMA_BACK)) / (SIGMA_BACK * math.sqrt(2.0 * math.pi))
    far = np.exp(-diff * diff / (2.0 * fog_sigma * fog_sigma)) / (fog_sigma * math.sqrt(2.0 * math.pi))
    return 0.5 * near + 0.5 * far


def two_terms(matrix):
    high = matrix.astype(ml_dtypes.bfloat16)
    low = (matrix - high.astype(np.float64)).astype(ml_dtypes.bfloat16)
    return high, low


def row_taps(count, scale):
    out_rows = np.arange(count, dtype=np.float64)[:, None]
    in_rows = np.arange(count + 2 * H, dtype=np.float64)[None, :]
    return np.concatenate(two_terms(scale * fine_taps(in_rows - H - out_rows)), axis=0)


def column_taps(scale):
    ins = np.arange(POOL + 2 * LANES, dtype=np.float64)[:, None] - LANES
    outs = np.arange(POOL, dtype=np.float64)[None, :]
    return two_terms(scale * fine_taps(ins - outs))


def split(value):
    high = value.astype(BF16)
    low = (value - high.astype(F32)).astype(BF16)
    return high, low


def dot(a, b):
    return jnp.dot(a, b, preferred_element_type=F32)


def blur_down(taps, rows):
    both = dot(taps, rows)
    half = both.shape[0] // 2
    return both[:half] + both[half:]


def blur_down3(taps, high, low):
    half = taps.shape[0] // 2
    both = dot(taps, high)
    return both[:half] + both[half:] + dot(taps[:half], low)


def blur_across(high, low, taps_high, taps_low):
    return dot(high, taps_high) + dot(high, taps_low) + dot(low, taps_high)


def levels(pattern):
    return jnp.where(pattern == 1, 5.0, jnp.where(pattern == 2, 7.0, 0.0)).astype(F32)


def signed_base(pattern):
    return jnp.where(pattern == 1, 1.5, jnp.where(pattern == 2, -1.95, 0.0)).astype(F32)


def less(base, forward):
    return jnp.where(base > 0, base - forward, jnp.where(base < 0, base + forward, 0.0))


def clear_rims(ref):
    zeros = jnp.zeros((ref.shape[0], LANES), BF16)
    ref[:, :LANES] = zeros
    ref[:, ref.shape[1] - LANES :] = zeros


def span(step):
    return pl.ds(pl.multiple_of(step * POOL, POOL), POOL + 2 * LANES)


def centre(step):
    return pl.ds(pl.multiple_of(step * POOL + LANES, LANES), POOL)


def first_kernel(steps, pattern_ref, big_ref, small_ref, wh_ref, wl_ref, out_ref, sums_ref, rh, rl, base_ref):
    step = pl.program_id(0)
    rows = pattern_ref.shape[0]
    big = big_ref.shape[1]
    wide = big - 2 * H
    slot = lax.rem(step, 2)

    @pl.when(step == 0)
    def _():
        clear_rims(rh)
        clear_rims(rl)

    @pl.when(step < steps)
    def _():
        pattern = pattern_ref[...]
        level = levels(pattern)
        x = level.astype(BF16)
        base_ref[slot] = signed_base(pattern)
        parts, at = [], 0
        while at + 2 * H < rows:
            taps = big_ref[...] if at + big <= rows else small_ref[...]
            parts.append((at, blur_down(taps, x[at : at + taps.shape[1]])))
            at += wide
        for at, part in parts:
            high, low = split(part)
            rh[at : at + part.shape[0], centre(step)] = high
            rl[at : at + part.shape[0], centre(step)] = low

    @pl.when(step > 0)
    def _():
        back = step - 1
        forward = blur_across(rh[:, span(back)], rl[:, span(back)], wh_ref[...], wl_ref[...])
        base = base_ref[1 - slot]
        now = less(base[H : rows - H], forward)
        out_ref[:H] = jnp.zeros((H, POOL), F32)
        out_ref[H : rows - H] = now
        out_ref[rows - H :] = jnp.zeros((H, POOL), F32)
        size = jnp.abs(now)
        sums = []
        for first, last in ((0, POOL - H), (POOL - H, rows - 2 * H)):
            sums.append(jnp.sum(size[first:last], axis=0, keepdims=True))
        level = jnp.where(base > 0, 5.0, jnp.where(base < 0, 7.0, 0.0))
        full = jnp.where(base != 0, 1.0, 0.0)
        for value in (level, full):
            for first in (0, POOL):
                sums.append(jnp.sum(value[first : first + POOL], axis=0, keepdims=True))
        sums.append(jnp.zeros((2, POOL), F32))
        sums_ref[...] = jnp.concatenate(sums, axis=0)


def edge_kernel(cells, ends_ref, above_ref, top_ref, bottom_ref, below_ref, sums_ref, taps_ref, wh_ref, wl_ref, edge_ref, send_ref):
    width = top_ref.shape[1]
    above = jnp.where(ends_ref[0] == 0, above_ref[...], 0)
    below = jnp.where(ends_ref[1] == 0, below_ref[...], 0)
    upper = jnp.concatenate([above, top_ref[...]], axis=0)
    lower = jnp.concatenate([bottom_ref[...], below], axis=0)
    blurred = [blur_down(taps_ref[...], levels(p).astype(BF16)) for p in (upper, lower)]
    rim = jnp.zeros((4 * H, LANES), BF16)
    wide = [jnp.concatenate([rim, part, rim], axis=1) for part in split(jnp.concatenate(blurred, axis=0))]
    stacked = [
        jnp.concatenate([w[:, POOL * j : POOL * (j + 1) + 2 * LANES] for j in range(cells)], axis=0) for w in wide
    ]
    forward = blur_across(stacked[0], stacked[1], wh_ref[...], wl_ref[...])
    base = signed_base(jnp.concatenate([upper[H : 3 * H], lower[H : 3 * H]], axis=0))
    row = lax.broadcasted_iota(jnp.int32, (8, LANES), 0)
    lane = lax.broadcasted_iota(jnp.int32, (8, LANES), 1)
    spread = jnp.zeros((8, LANES), F32)
    kind = lax.broadcasted_iota(jnp.int32, (8, POOL), 0)
    for j in range(cells):
        here = slice(POOL * j, POOL * (j + 1))
        now = less(base[:, here], forward[4 * H * j : 4 * H * (j + 1)])
        edge_ref[:, here] = now
        size = jnp.abs(now)
        top = jnp.sum(size[H : 2 * H], axis=0, keepdims=True)
        bottom = jnp.sum(size[2 * H : 3 * H], axis=0, keepdims=True)
        sums = sums_ref[:, here] + jnp.where(kind == 0, top, jnp.where(kind == 1, bottom, 0.0))
        total = jnp.sum(sums, axis=1, keepdims=True)
        spread = spread + jnp.where((lane == row * cells + j), total, 0.0)
    scale = jnp.where(row < 2, 1.0, jnp.where(row < 4, 0.2, 1.0)) / (POOL * POOL)
    send_ref[...] = jnp.broadcast_to(jnp.sum(spread * scale, axis=0, keepdims=True), send_ref.shape)


def exact_dot(a, b):
    return jnp.dot(a, b, precision=lax.Precision.HIGHEST, preferred_element_type=F32)


def back_kernel(cells, me_ref, all_ref, mix_ref, kernel_ref, out_ref, b1_ref):
    me = me_ref[0]
    count = all_ref.shape[0]
    pair = 2 * cells
    got = all_ref[...]
    adjusted = pltpu.roll(got, 0, 1)
    coarse = pltpu.roll(got, LANES - pair, 1)
    full = pltpu.roll(got, LANES - 2 * pair, 1)

    def mixed(value):
        three = exact_dot(value, mix_ref[...])
        return jnp.concatenate([three[:, LANES * i : LANES * (i + 1)] for i in range(3)], axis=0)

    b1 = exact_dot(kernel_ref[...], mixed(coarse))
    b1_ref[...] = b1
    second = adjusted - BACK_SHARE * b1 * full
    mine = jnp.broadcast_to(kernel_ref[pl.ds(me, 1), :], (8, 3 * count))
    b2 = exact_dot(mine, mixed(second))
    before = b1_ref[pl.ds(jnp.maximum(me - 1, 0), 1), :]
    here = b1_ref[pl.ds(me, 1), :]
    after = b1_ref[pl.ds(jnp.minimum(me + 1, count - 1), 1), :]
    own = b2[:1]
    lines = ((before, 1), (here, 0), (here, 1), (after, 0), (own, 0), (own, 1))
    for at, (value, half) in enumerate(lines):
        for j in range(cells):
            lane = half * cells + j
            out_ref[at : at + 1, POOL * j : POOL * (j + 1)] = jnp.broadcast_to(
                BACK_SHARE * value[:, lane : lane + 1], (1, POOL)
            )
    out_ref[6:8] = jnp.zeros((2, out_ref.shape[1]), F32)


def second_kernel(steps, now_ref, edge_ref, back_ref, last_ref, big_ref, small_ref, wh_ref, wl_ref, dose_ref, exposure_ref, rh, rl, base_ref):
    step = pl.program_id(0)
    rows = now_ref.shape[0]
    big = big_ref.shape[1]
    wide = big - 2 * H
    slot = lax.rem(step, 2)

    @pl.when(step == 0)
    def _():
        clear_rims(rh)
        clear_rims(rl)

    @pl.when(step < steps)
    def _():
        edge = edge_ref[...]
        pieces = [
            (edge[:H], 0),
            (edge[H : 2 * H], 1),
            (now_ref[H:POOL], 1),
            (now_ref[POOL : rows - H], 2),
            (edge[2 * H : 3 * H], 2),
            (edge[3 * H :], 3),
        ]
        doses, bases = [], []
        for value, line in pieces:
            level = jnp.where(value != 0, jnp.abs(value) - back_ref[line : line + 1], 0.0)
            doses.append(level)
            bases.append(jnp.where(value > 0, level + 0.5, jnp.where(value < 0, level + 0.55, 0.0)))
        base_ref[slot] = jnp.concatenate(bases[1:5], axis=0)
        high, low = split(jnp.concatenate(doses, axis=0))
        at = 0
        while at < rows:
            taps = big_ref[...] if at + big <= rows + 2 * H else small_ref[...]
            depth = taps.shape[1]
            part = blur_down3(taps, high[at : at + depth], low[at : at + depth])
            part_high, part_low = split(part)
            rh[at : at + part.shape[0], centre(step)] = part_high
            rl[at : at + part.shape[0], centre(step)] = part_low
            at += wide

    @pl.when(step > 0)
    def _():
        back = step - 1
        forward = blur_across(rh[:, span(back)], rl[:, span(back)], wh_ref[...], wl_ref[...])
        base = base_ref[1 - slot]
        own = jnp.concatenate(
            [jnp.broadcast_to(last_ref[4:5], (POOL, POOL)), jnp.broadcast_to(last_ref[5:6], (rows - POOL, POOL))], axis=0
        )
        exposure = forward + own
        exposure_ref[...] = exposure
        dose_ref[...] = jnp.where(base > 0, base - exposure, 0.0)


def whole(shape):
    return pl.BlockSpec(shape, lambda *_: (0,) * len(shape))


def local(pattern):
    rows, width = pattern.shape
    cells = width // POOL
    coarse_rows = rows // POOL
    count = lax.axis_size(AXES)
    me = lax.axis_index(AXES)
    fog_sigma = coarse_rows * count / 4.0
    wide = POOL - 2 * H
    params = functools.partial(pltpu.CompilerParams, vmem_limit_bytes=56 * 2**20)

    forward_ring = [(i, (i + 1) % count) for i in range(count)]
    backward_ring = [(j, i) for i, j in forward_ring]
    above = lax.ppermute(pattern[rows - 2 * H :], AXES, forward_ring)
    below = lax.ppermute(pattern[: 2 * H], AXES, backward_ring)

    taps_high, taps_low = (jnp.asarray(m) for m in column_taps(1.0 / TOTAL))
    column_spec = [whole(taps_high.shape)] * 2
    padded = width + 2 * LANES

    def at_step(step):
        return (0, jnp.minimum(step, cells - 1))

    def behind(step):
        return (0, jnp.maximum(step - 1, 0))

    big = jnp.asarray(row_taps(wide, 0.2))
    rest = (rows - 2 * H) % wide
    small = jnp.asarray(row_taps(rest, 0.2))
    now, sums = pl.pallas_call(
        functools.partial(first_kernel, cells),
        grid=(cells + 1,),
        in_specs=[pl.BlockSpec((rows, POOL), at_step), whole(big.shape), whole(small.shape)] + column_spec,
        out_specs=[pl.BlockSpec((rows, POOL), behind), pl.BlockSpec((8, POOL), behind)],
        out_shape=[jax.ShapeDtypeStruct((rows, width), F32), jax.ShapeDtypeStruct((8, width), F32)],
        scratch_shapes=[
            pltpu.VMEM((rows - 2 * H, padded), BF16),
            pltpu.VMEM((rows - 2 * H, padded), BF16),
            pltpu.VMEM((2, rows, POOL), F32),
        ],
        compiler_params=params(),
        cost_estimate=pl.CostEstimate(flops=6 * 10**9, bytes_accessed=3 * 10**7, transcendentals=0),
        name="first_blur",
    )(pattern, big, small, taps_high, taps_low)

    ends = jnp.stack([me == 0, me == count - 1]).astype(jnp.int32)
    edge_taps = jnp.asarray(row_taps(2 * H, 0.2))
    strip = (2 * H, width)
    last_block = rows // (2 * H) - 1
    edge, send = pl.pallas_call(
        functools.partial(edge_kernel, cells),
        grid=(1,),
        in_specs=[
            pl.BlockSpec(memory_space=pltpu.SMEM),
            whole(strip),
            whole(strip),
            pl.BlockSpec(strip, lambda i: (last_block, 0)),
            whole(strip),
            whole((8, width)),
            whole(edge_taps.shape),
        ]
        + column_spec,
        out_specs=[whole((4 * H, width)), whole((count, LANES))],
        out_shape=[jax.ShapeDtypeStruct((4 * H, width), F32), jax.ShapeDtypeStruct((count, LANES), F32)],
        compiler_params=params(),
        name="edge_blur",
    )(ends, above, pattern, pattern, below, sums, edge_taps, taps_high, taps_low)

    gathered = lax.all_to_all(send.reshape(count, 1, LANES), AXES, 0, 0, tiled=True).reshape(count, LANES)

    cols = np.arange(cells, dtype=np.float64)
    across = back_weight(cols[:, None] - cols[None, :], fog_sigma)
    mix = np.zeros((LANES, 3 * LANES))
    for half in range(2):
        mine = slice(half * cells, (half + 1) * cells)
        other = slice((1 - half) * cells, (2 - half) * cells)
        mix[mine, mine] = across
        where = LANES if half == 1 else 2 * LANES
        mix[mine, where + other.start : where + other.stop] = across
    strips = np.arange(count, dtype=np.float64)
    gap = 2.0 * (strips[None, :] - strips[:, None])
    down = np.concatenate([back_weight(gap + shift, fog_sigma) for shift in (0.0, 1.0, -1.0)], axis=1)
    back = pl.pallas_call(
        functools.partial(back_kernel, cells),
        grid=(1,),
        in_specs=[
            pl.BlockSpec(memory_space=pltpu.SMEM),
            whole((count, LANES)),
            whole(mix.shape),
            whole(down.shape),
        ],
        out_specs=whole((8, width)),
        out_shape=jax.ShapeDtypeStruct((8, width), F32),
        scratch_shapes=[pltpu.VMEM((count, LANES), F32)],
        compiler_params=params(),
        name="backscatter",
    )(me[None].astype(jnp.int32), gathered, jnp.asarray(mix.astype(np.float32)), jnp.asarray(down.astype(np.float32)))

    big = jnp.asarray(row_taps(wide, 1.0))
    rest = rows % wide
    small = jnp.asarray(row_taps(rest, 1.0))
    return pl.pallas_call(
        functools.partial(second_kernel, cells),
        grid=(cells + 1,),
        in_specs=[
            pl.BlockSpec((rows, POOL), at_step),
            pl.BlockSpec((4 * H, POOL), at_step),
            pl.BlockSpec((8, POOL), at_step),
            pl.BlockSpec((8, POOL), behind),
            whole(big.shape),
            whole(small.shape),
        ]
        + column_spec,
        out_specs=[pl.BlockSpec((rows, POOL), behind)] * 2,
        out_shape=[jax.ShapeDtypeStruct((rows, width), F32)] * 2,
        scratch_shapes=[
            pltpu.VMEM((rows, padded), BF16),
            pltpu.VMEM((rows, padded), BF16),
            pltpu.VMEM((2, rows, POOL), F32),
        ],
        compiler_params=params(),
        cost_estimate=pl.CostEstimate(flops=8 * 10**9, bytes_accessed=3 * 10**7, transcendentals=0),
        name="second_blur",
    )(now, edge, back, back, big, small, taps_high, taps_low)


def solution(mesh):
    return jax.shard_map(
        local,
        mesh=mesh,
        in_specs=(P(AXES, None),),
        out_specs=(P(AXES, None), P(AXES, None)),
        check_vma=False,
    )
```

```python
import functools
import math

import jax
import jax.numpy as jnp
import ml_dtypes
import numpy as np
from jax import lax
from jax.experimental import pallas as pl
from jax.experimental.pallas import tpu as pltpu
from jax.sharding import PartitionSpec as P

POOL = 256
H = 16
ETA_BACK = 0.75
SIGMA_BACK = 6.0
TOTAL = 1.0 + ETA_BACK
BACK_SHARE = ETA_BACK / TOTAL
AXES = ("band", "strip")
F32 = jnp.float32
BF16 = jnp.bfloat16
LANES = 128


def fine_taps(diff):
    spread = H / 3.0
    steps = np.arange(-H, H + 1, dtype=np.float64)
    total = np.exp(-steps * steps / (2.0 * spread * spread)).sum()
    weight = np.exp(-diff * diff / (2.0 * spread * spread)) / total
    return np.where(np.abs(diff) <= H, weight, 0.0)


def back_weight(diff, fog_sigma):
    near = np.exp(-diff * diff / (2.0 * SIGMA_BACK * SIGMA_BACK)) / (SIGMA_BACK * math.sqrt(2.0 * math.pi))
    far = np.exp(-diff * diff / (2.0 * fog_sigma * fog_sigma)) / (fog_sigma * math.sqrt(2.0 * math.pi))
    return 0.5 * near + 0.5 * far


def two_terms(matrix):
    high = matrix.astype(ml_dtypes.bfloat16)
    low = (matrix - high.astype(np.float64)).astype(ml_dtypes.bfloat16)
    return high, low


def row_taps(count, scale):
    out_rows = np.arange(count, dtype=np.float64)[:, None]
    in_rows = np.arange(count + 2 * H, dtype=np.float64)[None, :]
    return np.concatenate(two_terms(scale * fine_taps(in_rows - H - out_rows)), axis=0)


def column_taps(scale):
    ins = np.arange(POOL + 2 * LANES, dtype=np.float64)[:, None] - LANES
    outs = np.arange(POOL, dtype=np.float64)[None, :]
    return two_terms(scale * fine_taps(ins - outs))


def split(value):
    high = value.astype(BF16)
    low = (value - high.astype(F32)).astype(BF16)
    return high, low


def dot(a, b):
    return jnp.dot(a, b, preferred_element_type=F32)


def blur_down(taps, rows):
    both = dot(taps, rows)
    half = both.shape[0] // 2
    return both[:half] + both[half:]


def blur_down3(taps, high, low):
    half = taps.shape[0] // 2
    both = dot(taps, high)
    return both[:half] + both[half:] + dot(taps[:half], low)


def blur_across(high, low, taps_high, taps_low):
    return dot(high, taps_high) + dot(high, taps_low) + dot(low, taps_high)


def clear_rims(ref):
    zeros = jnp.zeros((ref.shape[0], LANES), BF16)
    ref[:, :LANES] = zeros
    ref[:, ref.shape[1] - LANES :] = zeros


def pixels(pattern):
    kind = pattern.astype(F32)
    return kind, jnp.where(pattern == 2, 7.0, 5.0 * kind)


LIFT = 1.05
MIDDLE = 1.85


def column_sums(value):
    return jnp.sum(value, axis=0, keepdims=True)


def rims_kernel(pattern_hbm, odd_ref, even_ref, sem):
    rows, rim = pattern_hbm.shape[0], odd_ref.shape[0]
    last = rows - rim
    odd = lax.rem(lax.axis_index(AXES), 2)
    copies = [
        pltpu.make_async_copy(pattern_hbm.at[pl.ds(pl.multiple_of(start, rim), rim)], ref, sem.at[i])
        for i, (ref, start) in enumerate(((odd_ref, odd * last), (even_ref, (1 - odd) * last)))
    ]
    for copy in copies:
        copy.start()
    for copy in copies:
        copy.wait()


def first_kernel(
    pattern_hbm, big_hbm, small_hbm, wh_hbm, wl_hbm, out_hbm, sums_ref,
    pattern_ref, out_ref, big_ref, small_ref, wh_ref, wl_ref, rh, rl, in_sem, out_sem, taps_sem,
):
    rows, width = pattern_ref.shape
    cells = width // POOL
    big = big_ref.shape[1]
    wide = big - 2 * H

    def cell(t):
        return slice(POOL * t, POOL * (t + 1))

    loads = [pltpu.make_async_copy(pattern_hbm.at[:, cell(t)], pattern_ref.at[:, cell(t)], in_sem.at[t]) for t in range(cells)]
    stores = [pltpu.make_async_copy(out_ref.at[:, cell(t)], out_hbm.at[:, cell(t)], out_sem.at[t]) for t in range(cells)]
    pairs = ((big_hbm, big_ref), (small_hbm, small_ref), (wh_hbm, wh_ref), (wl_hbm, wl_ref))
    taps_loads = [pltpu.make_async_copy(hbm, ref, taps_sem.at[i]) for i, (hbm, ref) in enumerate(pairs)]
    for load in loads[:1] + taps_loads + loads[1:]:
        load.start()
    clear_rims(rh)
    clear_rims(rl)
    for load in taps_loads:
        load.wait()

    def down(t):
        here = slice(POOL * t + LANES, POOL * (t + 1) + LANES)
        _, level = pixels(pattern_ref[:, cell(t)])
        x = level.astype(BF16)
        at = 0
        while at + 2 * H < rows:
            taps = big_ref[...] if at + big <= rows else small_ref[...]
            part = blur_down(taps, x[at : at + taps.shape[1]])
            rh[at : at + part.shape[0], here], rl[at : at + part.shape[0], here] = split(part)
            at += wide

    def across(t):
        window = slice(POOL * t, POOL * (t + 1) + 2 * LANES)
        forward = blur_across(rh[:, window], rl[:, window], wh_ref[...], wl_ref[...])
        kind, level = pixels(pattern_ref[:, cell(t)])
        now = jnp.maximum(1.5 * kind[H : rows - H] - forward, 0.0)
        zeros = jnp.zeros((H, POOL), F32)
        out_ref[:H, cell(t)] = zeros
        out_ref[H : rows - H, cell(t)] = now
        out_ref[rows - H :, cell(t)] = zeros
        sums = [column_sums(now[: POOL - H]), column_sums(now[POOL - H :])]
        sums += [column_sums(value[first : first + POOL]) for value in (level, kind) for first in (0, POOL)]
        sums_ref[:, cell(t)] = jnp.concatenate(sums + [jnp.zeros((2, POOL), F32)], axis=0)
        stores[t].start()

    for t in range(cells + 1):
        if t < cells:
            loads[t].wait()
            down(t)
        if t > 0:
            across(t - 1)
    for store in stores:
        store.wait()


def edge_kernel(for_odd_ref, for_even_ref, from_odd_ref, from_even_ref, sums_ref, taps_ref, wh_ref, wl_ref, edge_ref, send_ref):
    count = lax.axis_size(AXES)
    me = lax.axis_index(AXES)
    width = edge_ref.shape[1]
    cells = width // POOL
    even = lax.rem(me, 2) == 0
    top = jnp.where(even, for_odd_ref[...], for_even_ref[...])
    bottom = jnp.where(even, for_even_ref[...], for_odd_ref[...])
    above = jnp.where(even, from_odd_ref[...], from_even_ref[...])
    below = jnp.where(even, from_even_ref[...], from_odd_ref[...])
    above = jnp.where(me > 0, above, 0)
    below = jnp.where(me < count - 1, below, 0)
    upper = jnp.concatenate([above, top], axis=0)
    lower = jnp.concatenate([bottom, below], axis=0)
    blurred = [blur_down(taps_ref[...], pixels(p)[1].astype(BF16)) for p in (upper, lower)]
    rim = jnp.zeros((4 * H, LANES), BF16)
    wide = [jnp.concatenate([rim, part, rim], axis=1) for part in split(jnp.concatenate(blurred, axis=0))]
    stacked = [
        jnp.concatenate([w[:, POOL * j : POOL * (j + 1) + 2 * LANES] for j in range(cells)], axis=0) for w in wide
    ]
    forward = blur_across(stacked[0], stacked[1], wh_ref[...], wl_ref[...])
    kind = jnp.concatenate([upper[H : 3 * H], lower[H : 3 * H]], axis=0).astype(F32)
    row = lax.broadcasted_iota(jnp.int32, (8, POOL), 0)
    place = lax.broadcasted_iota(jnp.int32, (8, LANES), 0)
    lane = lax.broadcasted_iota(jnp.int32, (8, LANES), 1)
    spread = jnp.zeros((8, LANES), F32)
    for j in range(cells):
        here = slice(POOL * j, POOL * (j + 1))
        now = jnp.maximum(1.5 * kind[:, here] - forward[4 * H * j : 4 * H * (j + 1)], 0.0)
        edge_ref[:, here] = now
        top, bottom = column_sums(now[H : 2 * H]), column_sums(now[2 * H : 3 * H])
        sums = sums_ref[:, here] + jnp.where(row == 0, top, jnp.where(row == 1, bottom, 0.0))
        total = jnp.sum(sums, axis=1, keepdims=True)
        value, fifths, classes = total[0:2], total[2:4], total[4:6]
        second = (5.0 * classes - fifths) * (1.0 / 3.0)
        total = jnp.concatenate([value - LIFT * second, 0.2 * fifths, classes - second, jnp.zeros((2, 1), F32)], axis=0)
        spread = spread + jnp.where(lane == place * cells + j, total, 0.0)
    line = column_sums(spread) * (1.0 / (POOL * POOL))
    send_ref[...] = jnp.broadcast_to(line, send_ref.shape)


def product(a, b):
    return dot(a[0], b[0]) + dot(a[1], b[0]) + dot(a[0], b[1])


def find_back(me, all_ref, mix, kernel, up_ref, b1_ref, b2_ref):
    count = all_ref.shape[0]
    cells = up_ref.shape[1] // POOL
    pair = 2 * cells
    adjusted = all_ref[...]
    coarse = pltpu.roll(adjusted, LANES - pair, 1)
    full = pltpu.roll(adjusted, LANES - 2 * pair, 1)

    def scatter(value):
        three = product(split(value), mix)
        return product(kernel, split(jnp.concatenate([three[:, LANES * i : LANES * (i + 1)] for i in range(3)], axis=0)))

    b1 = scatter(coarse)
    b1_ref[...] = b1
    b2_ref[...] = scatter(adjusted - BACK_SHARE * b1 * full)
    before = b1_ref[pl.ds(jnp.maximum(me - 1, 0), 1), :]
    here = b1_ref[pl.ds(me, 1), :]
    after = b1_ref[pl.ds(jnp.minimum(me + 1, count - 1), 1), :]
    own = b2_ref[pl.ds(me, 1), :]
    for at, (value, half) in enumerate(((before, 1), (here, 0), (here, 1), (after, 0), (own, 0), (own, 1))):
        value = BACK_SHARE * value
        for j in range(cells):
            lane = half * cells + j
            up_ref[at : at + 1, POOL * j : POOL * (j + 1)] = jnp.broadcast_to(value[:, lane : lane + 1], (1, POOL))


def second_kernel(
    now_hbm, edge_ref, all_ref, mixh_ref, mixl_ref, kerh_ref, kerl_ref, big_ref, small_ref, wh_ref, wl_ref,
    dose_hbm, exposure_hbm,
    now_ref, dose_ref, exposure_ref, rh, rl, up_ref, b1_ref, b2_ref, in_sem, dose_sem, exposure_sem,
):
    rows, width = now_ref.shape
    cells = width // POOL
    big = big_ref.shape[1]
    wide = big - 2 * H

    def cell(t):
        return slice(POOL * t, POOL * (t + 1))

    loads = [pltpu.make_async_copy(now_hbm.at[:, cell(t)], now_ref.at[:, cell(t)], in_sem.at[t]) for t in range(cells)]
    stores = [
        [pltpu.make_async_copy(ref.at[:, cell(t)], hbm.at[:, cell(t)], sem.at[t]) for t in range(cells)]
        for ref, hbm, sem in ((dose_ref, dose_hbm, dose_sem), (exposure_ref, exposure_hbm, exposure_sem))
    ]
    for load in loads:
        load.start()
    clear_rims(rh)
    clear_rims(rl)
    find_back(
        lax.axis_index(AXES), all_ref, (mixh_ref[...], mixl_ref[...]), (kerh_ref[...], kerl_ref[...]), up_ref, b1_ref, b2_ref
    )

    def down(t):
        here = slice(POOL * t + LANES, POOL * (t + 1) + LANES)
        edge = edge_ref[:, cell(t)]
        pieces = [
            (edge[:H], 0),
            (edge[H : 2 * H], 1),
            (now_ref[H:POOL, cell(t)], 1),
            (now_ref[POOL : rows - H, cell(t)], 2),
            (edge[2 * H : 3 * H], 2),
            (edge[3 * H :], 3),
        ]
        doses, at = [], -H
        for value, line in pieces:
            second = value > MIDDLE
            dose = value - up_ref[line : line + 1, cell(t)]
            dose = jnp.maximum(jnp.where(second, dose - LIFT, dose), 0.0)
            doses.append(dose)
            if 0 <= at < rows:
                base = jnp.where(dose > 0, dose + jnp.where(second, 0.55, 0.5), 0.0)
                dose_ref[at : at + value.shape[0], cell(t)] = base
            at += value.shape[0]
        high, low = split(jnp.concatenate(doses, axis=0))
        at = 0
        while at < rows:
            taps = big_ref[...] if at + big <= rows + 2 * H else small_ref[...]
            depth = taps.shape[1]
            part = blur_down3(taps, high[at : at + depth], low[at : at + depth])
            rh[at : at + part.shape[0], here], rl[at : at + part.shape[0], here] = split(part)
            at += wide

    def across(t):
        window = slice(POOL * t, POOL * (t + 1) + 2 * LANES)
        forward = blur_across(rh[:, window], rl[:, window], wh_ref[...], wl_ref[...])
        for half in range(rows // POOL):
            these = slice(POOL * half, POOL * (half + 1))
            exposure = forward[these] + up_ref[4 + half : 5 + half, cell(t)]
            base = dose_ref[these, cell(t)]
            exposure_ref[these, cell(t)] = exposure
            dose_ref[these, cell(t)] = jnp.where(base > 0, base - exposure, 0.0)
        for group in stores:
            group[t].start()

    for t in range(cells + 1):
        if t < cells:
            loads[t].wait()
            down(t)
        if t > 0:
            across(t - 1)
    for group in stores:
        for store in group:
            store.wait()


VMEM = pl.BlockSpec(memory_space=pltpu.VMEM)
HBM = pl.BlockSpec(memory_space=pltpu.HBM)


def local(pattern):
    rows, width = pattern.shape
    cells = width // POOL
    coarse_rows = rows // POOL
    count = lax.axis_size(AXES)
    fog_sigma = coarse_rows * count / 4.0
    wide = POOL - 2 * H
    padded = width + 2 * LANES
    def params(mebibytes):
        return pltpu.CompilerParams(vmem_limit_bytes=mebibytes * 2**20)

    odd_pairs = [(i, i if i in (0, count - 1) else ((i + 1) ^ 1) - 1) for i in range(count)]
    even_pairs = [(i, i ^ 1) for i in range(count)]
    for_odd, for_even = pl.pallas_call(
        rims_kernel,
        in_specs=[HBM],
        out_specs=[VMEM] * 2,
        out_shape=[jax.ShapeDtypeStruct((2 * H, width), pattern.dtype)] * 2,
        scratch_shapes=[pltpu.SemaphoreType.DMA((2,))],
        name="rims",
    )(pattern)
    from_odd = lax.ppermute(for_odd, AXES, odd_pairs)
    from_even = lax.ppermute(for_even, AXES, even_pairs)

    taps_high, taps_low = (jnp.asarray(m) for m in column_taps(1.0 / TOTAL))

    big = jnp.asarray(row_taps(wide, 0.2))
    small = jnp.asarray(row_taps((rows - 2 * H) % wide, 0.2))
    now, sums = pl.pallas_call(
        first_kernel,
        in_specs=[HBM] * 5,
        out_specs=[HBM, VMEM],
        out_shape=[jax.ShapeDtypeStruct((rows, width), F32), jax.ShapeDtypeStruct((8, width), F32)],
        scratch_shapes=[pltpu.VMEM((rows, width), jnp.int32), pltpu.VMEM((rows, width), F32)]
        + [pltpu.VMEM(m.shape, BF16) for m in (big, small, taps_high, taps_low)]
        + [pltpu.VMEM((rows - 2 * H, padded), BF16)] * 2
        + [pltpu.SemaphoreType.DMA((cells,))] * 2
        + [pltpu.SemaphoreType.DMA((4,))],
        compiler_params=params(52),
        cost_estimate=pl.CostEstimate(flops=6 * 10**9, bytes_accessed=3 * 10**7, transcendentals=0),
        name="first_blur",
    )(pattern, big, small, taps_high, taps_low)

    edge_taps = jnp.asarray(row_taps(2 * H, 0.2))
    edge, send = pl.pallas_call(
        edge_kernel,
        in_specs=[VMEM] * 8,
        out_specs=[VMEM] * 2,
        out_shape=[jax.ShapeDtypeStruct((4 * H, width), F32), jax.ShapeDtypeStruct((count, LANES), F32)],
        compiler_params=params(40),
        name="edge_blur",
    )(for_odd, for_even, from_odd, from_even, sums, edge_taps, taps_high, taps_low)

    gathered = lax.all_to_all(send.reshape(count, 1, LANES), AXES, 0, 0, tiled=True).reshape(count, LANES)

    cols = np.arange(cells, dtype=np.float64)
    across = back_weight(cols[:, None] - cols[None, :], fog_sigma)
    mix = np.zeros((LANES, 3 * LANES))
    for half in range(2):
        mine = slice(half * cells, (half + 1) * cells)
        other = slice((1 - half) * cells, (2 - half) * cells)
        mix[mine, mine] = across
        where = LANES if half == 1 else 2 * LANES
        mix[mine, where + other.start : where + other.stop] = across
    strips = np.arange(count, dtype=np.float64)
    gap = 2.0 * (strips[None, :] - strips[:, None])
    down = np.concatenate([back_weight(gap + shift, fog_sigma) for shift in (0.0, 1.0, -1.0)], axis=1)
    constants = [jnp.asarray(m) for m in two_terms(mix) + two_terms(down)]

    big = jnp.asarray(row_taps(wide, 1.0))
    small = jnp.asarray(row_taps(rows % wide, 1.0))
    return pl.pallas_call(
        second_kernel,
        in_specs=[HBM] + [VMEM] * 10,
        out_specs=[HBM] * 2,
        out_shape=[jax.ShapeDtypeStruct((rows, width), F32)] * 2,
        scratch_shapes=[pltpu.VMEM((rows, width), F32)] * 3
        + [pltpu.VMEM((rows, padded), BF16)] * 2
        + [pltpu.VMEM((8, width), F32)]
        + [pltpu.VMEM((count, LANES), F32)] * 2
        + [pltpu.SemaphoreType.DMA((cells,))] * 3,
        compiler_params=params(50),
        cost_estimate=pl.CostEstimate(flops=8 * 10**9, bytes_accessed=3 * 10**7, transcendentals=0),
        name="second_blur",
    )(now, edge, gathered, *constants, big, small, taps_high, taps_low)


def solution(mesh):
    return jax.shard_map(
        local,
        mesh=mesh,
        in_specs=(P(AXES, None),),
        out_specs=(P(AXES, None), P(AXES, None)),
        check_vma=False,
    )
```

```python
import functools
import math

import jax
import jax.numpy as jnp
import ml_dtypes
import numpy as np
from jax import lax
from jax.experimental import pallas as pl
from jax.experimental.pallas import tpu as pltpu
from jax.sharding import PartitionSpec as P

POOL = 256
H = 16
ETA_BACK = 0.75
SIGMA_BACK = 6.0
TOTAL = 1.0 + ETA_BACK
BACK_SHARE = ETA_BACK / TOTAL
AXES = ("band", "strip")
F32 = jnp.float32
BF16 = jnp.bfloat16
LANES = 128


def fine_taps(diff):
    spread = H / 3.0
    steps = np.arange(-H, H + 1, dtype=np.float64)
    total = np.exp(-steps * steps / (2.0 * spread * spread)).sum()
    weight = np.exp(-diff * diff / (2.0 * spread * spread)) / total
    return np.where(np.abs(diff) <= H, weight, 0.0)


def back_weight(diff, fog_sigma):
    near = np.exp(-diff * diff / (2.0 * SIGMA_BACK * SIGMA_BACK)) / (SIGMA_BACK * math.sqrt(2.0 * math.pi))
    far = np.exp(-diff * diff / (2.0 * fog_sigma * fog_sigma)) / (fog_sigma * math.sqrt(2.0 * math.pi))
    return 0.5 * near + 0.5 * far


def two_terms(matrix):
    high = matrix.astype(ml_dtypes.bfloat16)
    low = (matrix - high.astype(np.float64)).astype(ml_dtypes.bfloat16)
    return high, low


def row_taps(count, scale):
    out_rows = np.arange(count, dtype=np.float64)[:, None]
    in_rows = np.arange(count + 2 * H, dtype=np.float64)[None, :]
    return np.concatenate(two_terms(scale * fine_taps(in_rows - H - out_rows)), axis=0)


def column_taps(scale):
    ins = np.arange(POOL + 2 * LANES, dtype=np.float64)[:, None] - LANES
    outs = np.arange(POOL, dtype=np.float64)[None, :]
    return two_terms(scale * fine_taps(ins - outs))


def split(value):
    high = value.astype(BF16)
    low = (value - high.astype(F32)).astype(BF16)
    return high, low


def dot(a, b):
    return jnp.dot(a, b, preferred_element_type=F32)


def blur_down(taps, rows):
    both = dot(taps, rows)
    half = both.shape[0] // 2
    return both[:half] + both[half:]


def blur_down3(taps, high, low):
    half = taps.shape[0] // 2
    both = dot(taps, high)
    return both[:half] + both[half:] + dot(taps[:half], low)


def blur_across(high, low, taps_high, taps_low):
    return dot(high, taps_high) + dot(high, taps_low) + dot(low, taps_high)


def clear_rims(ref):
    zeros = jnp.zeros((ref.shape[0], LANES), BF16)
    ref[:, :LANES] = zeros
    ref[:, ref.shape[1] - LANES :] = zeros


def pixels(pattern):
    kind = pattern.astype(F32)
    return kind, jnp.where(pattern == 2, 7.0, 5.0 * kind)


LIFT = 1.05
MIDDLE = 1.85


def column_sums(value):
    return jnp.sum(value, axis=0, keepdims=True)


def windows(first, last, wide):
    return [(at, min(at + wide, last)) for at in range(first, last, wide)]


def rims_kernel(pattern_ref, odd_ref, even_ref):
    even = lax.rem(lax.axis_index(AXES), 2) == 0
    top, bottom = pattern_ref[: 2 * H], pattern_ref[pattern_ref.shape[0] - 2 * H :]
    odd_ref[...] = jnp.where(even, top, bottom)
    even_ref[...] = jnp.where(even, bottom, top)


def cut(packed_ref):
    column = POOL + 2 * LANES
    tall = 2 * (POOL - 2 * H)
    at = 2 * column + tall
    return packed_ref[:column], packed_ref[column : 2 * column], packed_ref[2 * column : at], packed_ref[at : at + 4 * H, : 4 * H]


def first_kernel(pattern_ref, taps_ref, out_ref, sums_ref, rh, rl):
    wh, wl, big, small = cut(taps_ref)
    rows, width = pattern_ref.shape
    cells = width // POOL
    clear_rims(rh)
    clear_rims(rl)
    parts = windows(H, rows - H, big.shape[1] - 2 * H)
    zeros = jnp.zeros((H, width), F32)
    out_ref[:H] = zeros
    out_ref[rows - H :] = zeros

    def cell(t):
        return slice(POOL * t, POOL * (t + 1))

    def down(t):
        here = slice(POOL * t + LANES, POOL * (t + 1) + LANES)
        _, level = pixels(pattern_ref[:, cell(t)])
        x = level.astype(BF16)
        for first, last in parts:
            taps = big if last - first + 2 * H == big.shape[1] else small
            part = blur_down(taps, x[first - H : last + H])
            rh[first - H : last - H, here], rl[first - H : last - H, here] = split(part)

    def across(t):
        window = slice(POOL * t, POOL * (t + 1) + 2 * LANES)
        forward = blur_across(rh[:, window], rl[:, window], wh, wl)
        kind, level = pixels(pattern_ref[:, cell(t)])
        now = jnp.maximum(1.5 * kind[H : rows - H] - forward, 0.0)
        out_ref[H : rows - H, cell(t)] = now
        sums = [column_sums(now[: POOL - H]), column_sums(now[POOL - H :])]
        sums += [column_sums(value[first : first + POOL]) for value in (level, kind) for first in (0, POOL)]
        sums_ref[:, cell(t)] = jnp.concatenate(sums + [jnp.zeros((2, POOL), F32)], axis=0)

    for t in range(cells + 1):
        if t < cells:
            down(t)
        if t > 0:
            across(t - 1)


def edge_kernel(for_odd_ref, for_even_ref, from_odd_ref, from_even_ref, sums_ref, taps_ref, edge_ref, send_ref):
    count = lax.axis_size(AXES)
    me = lax.axis_index(AXES)
    width = edge_ref.shape[1]
    wh, wl, _, taps = cut(taps_ref)
    cells = width // POOL
    even = lax.rem(me, 2) == 0
    top = jnp.where(even, for_odd_ref[...], for_even_ref[...])
    bottom = jnp.where(even, for_even_ref[...], for_odd_ref[...])
    above = jnp.where(even, from_odd_ref[...], from_even_ref[...])
    below = jnp.where(even, from_even_ref[...], from_odd_ref[...])
    above = jnp.where(me > 0, above, 0)
    below = jnp.where(me < count - 1, below, 0)
    upper = jnp.concatenate([above, top], axis=0)
    lower = jnp.concatenate([bottom, below], axis=0)
    blurred = [blur_down(taps, pixels(p)[1].astype(BF16)) for p in (upper, lower)]
    rim = jnp.zeros((4 * H, LANES), BF16)
    wide = [jnp.concatenate([rim, part, rim], axis=1) for part in split(jnp.concatenate(blurred, axis=0))]
    stacked = [
        jnp.concatenate([w[:, POOL * j : POOL * (j + 1) + 2 * LANES] for j in range(cells)], axis=0) for w in wide
    ]
    forward = blur_across(stacked[0], stacked[1], wh, wl)
    kind = jnp.concatenate([upper[H : 3 * H], lower[H : 3 * H]], axis=0).astype(F32)
    row = lax.broadcasted_iota(jnp.int32, (8, POOL), 0)
    place = lax.broadcasted_iota(jnp.int32, (8, LANES), 0)
    lane = lax.broadcasted_iota(jnp.int32, (8, LANES), 1)
    spread = jnp.zeros((8, LANES), F32)
    for j in range(cells):
        here = slice(POOL * j, POOL * (j + 1))
        now = jnp.maximum(1.5 * kind[:, here] - forward[4 * H * j : 4 * H * (j + 1)], 0.0)
        edge_ref[:, here] = now
        top, bottom = column_sums(now[H : 2 * H]), column_sums(now[2 * H : 3 * H])
        sums = sums_ref[:, here] + jnp.where(row == 0, top, jnp.where(row == 1, bottom, 0.0))
        total = jnp.sum(sums, axis=1, keepdims=True)
        value, fifths, classes = total[0:2], total[2:4], total[4:6]
        second = (5.0 * classes - fifths) * (1.0 / 3.0)
        total = jnp.concatenate([value - LIFT * second, 0.2 * fifths, classes - second, jnp.zeros((2, 1), F32)], axis=0)
        spread = spread + jnp.where(lane == place * cells + j, total, 0.0)
    line = column_sums(spread) * (1.0 / (POOL * POOL))
    send_ref[...] = jnp.broadcast_to(line, send_ref.shape)


def product(a, b):
    return dot(a[0], b[0]) + dot(a[1], b[0]) + dot(a[0], b[1])


def find_back(me, all_ref, mix, kernel, up_ref, b1_ref, b2_ref):
    count = all_ref.shape[0]
    cells = up_ref.shape[1] // POOL
    pair = 2 * cells
    adjusted = all_ref[...]
    coarse = pltpu.roll(adjusted, LANES - pair, 1)
    full = pltpu.roll(adjusted, LANES - 2 * pair, 1)

    def scatter(value):
        three = product(split(value), mix)
        return product(kernel, split(jnp.concatenate([three[:, LANES * i : LANES * (i + 1)] for i in range(3)], axis=0)))

    b1 = scatter(coarse)
    b1_ref[...] = b1
    b2_ref[...] = scatter(adjusted - BACK_SHARE * b1 * full)
    before = b1_ref[pl.ds(jnp.maximum(me - 1, 0), 1), :]
    here = b1_ref[pl.ds(me, 1), :]
    after = b1_ref[pl.ds(jnp.minimum(me + 1, count - 1), 1), :]
    own = b2_ref[pl.ds(me, 1), :]
    for at, (value, half) in enumerate(((before, 1), (here, 0), (here, 1), (after, 0), (own, 0), (own, 1))):
        value = BACK_SHARE * value
        for j in range(cells):
            lane = half * cells + j
            up_ref[at : at + 1, POOL * j : POOL * (j + 1)] = jnp.broadcast_to(value[:, lane : lane + 1], (1, POOL))


def second_kernel(
    now_ref, edge_ref, all_ref, mixh_ref, mixl_ref, kerh_ref, kerl_ref, big_ref, small_ref, wh_ref, wl_ref,
    dose_hbm, exposure_hbm,
    dose_ref, exposure_ref, rh, rl, up_ref, b1_ref, b2_ref, dose_sem, exposure_sem,
):
    rows, width = now_ref.shape
    cells = width // POOL
    big = big_ref.shape[1]
    wide = big - 2 * H

    def cell(t):
        return slice(POOL * t, POOL * (t + 1))

    parts = windows(0, rows, wide)
    stores = [
        [pltpu.make_async_copy(ref.at[a:b], hbm.at[a:b], sem.at[i]) for i, (a, b) in enumerate(parts)]
        for ref, hbm, sem in ((dose_ref, dose_hbm, dose_sem), (exposure_ref, exposure_hbm, exposure_sem))
    ]
    clear_rims(rh)
    clear_rims(rl)
    find_back(
        lax.axis_index(AXES), all_ref, (mixh_ref[...], mixl_ref[...]), (kerh_ref[...], kerl_ref[...]), up_ref, b1_ref, b2_ref
    )

    runs = [
        (-H, 0, edge_ref, 0, 0),
        (0, H, edge_ref, H, 1),
        (H, POOL, now_ref, H, 1),
        (POOL, rows - H, now_ref, POOL, 2),
        (rows - H, rows, edge_ref, 2 * H, 2),
        (rows, rows + H, edge_ref, 3 * H, 3),
    ]

    def dose_rows(first, last, t):
        doses = []
        for start, stop, ref, at, line in runs:
            a, b = max(start, first), min(stop, last)
            if a >= b:
                continue
            value = ref[at + a - start : at + b - start, cell(t)]
            second = value > MIDDLE
            dose = value - up_ref[line : line + 1, cell(t)]
            dose = jnp.maximum(jnp.where(second, dose - LIFT, dose), 0.0)
            doses.append(dose)
            low, high = max(a, first + H), min(b, last - H)
            if low < high:
                base = jnp.where(dose > 0, dose + jnp.where(second, 0.55, 0.5), 0.0)
                dose_ref[low:high, cell(t)] = base[low - a : high - a]
        return jnp.concatenate(doses, axis=0)

    for i, (first, last) in enumerate(parts):
        taps = big_ref[...] if last - first == wide else small_ref[...]
        for t in range(cells + 1):
            if t < cells:
                here = slice(POOL * t + LANES, POOL * (t + 1) + LANES)
                part = blur_down3(taps, *split(dose_rows(first - H, last + H, t)))
                rh[first:last, here], rl[first:last, here] = split(part)
            if t > 0:
                here = cell(t - 1)
                window = slice(POOL * (t - 1), POOL * t + 2 * LANES)
                forward = blur_across(rh[first:last, window], rl[first:last, window], wh_ref[...], wl_ref[...])
                for half in range(rows // POOL):
                    a, b = max(first, POOL * half), min(last, POOL * (half + 1))
                    if a >= b:
                        continue
                    exposure = forward[a - first : b - first] + up_ref[4 + half : 5 + half, here]
                    base = dose_ref[a:b, here]
                    exposure_ref[a:b, here] = exposure
                    dose_ref[a:b, here] = jnp.where(base > 0, base - exposure, 0.0)
        for group in stores:
            group[i].start()
    for group in stores:
        for store in group:
            store.wait()


VMEM = pl.BlockSpec(memory_space=pltpu.VMEM)
HBM = pl.BlockSpec(memory_space=pltpu.HBM)


def local(pattern):
    rows, width = pattern.shape
    cells = width // POOL
    coarse_rows = rows // POOL
    count = lax.axis_size(AXES)
    fog_sigma = coarse_rows * count / 4.0
    wide = POOL - 2 * H
    padded = width + 2 * LANES
    def params(mebibytes):
        return pltpu.CompilerParams(vmem_limit_bytes=mebibytes * 2**20)

    odd_pairs = [(i, i if i in (0, count - 1) else ((i + 1) ^ 1) - 1) for i in range(count)]
    even_pairs = [(i, i ^ 1) for i in range(count)]
    for_odd, for_even = pl.pallas_call(
        rims_kernel,
        in_specs=[VMEM],
        out_specs=[VMEM] * 2,
        out_shape=[jax.ShapeDtypeStruct((2 * H, width), pattern.dtype)] * 2,
        compiler_params=params(40),
        name="rims",
    )(pattern)
    from_odd = lax.ppermute(for_odd, AXES, odd_pairs)
    from_even = lax.ppermute(for_even, AXES, even_pairs)

    taps_high, taps_low = (jnp.asarray(m) for m in column_taps(1.0 / TOTAL))

    assert (rows - 2 * H) % wide in (0, 2 * H)
    short = row_taps(2 * H, 0.2)
    short = np.concatenate([short, np.zeros((short.shape[0], POOL - short.shape[1]), short.dtype)], axis=1)
    first_taps = jnp.asarray(np.concatenate([*column_taps(1.0 / TOTAL), row_taps(wide, 0.2), short], axis=0))
    now, sums = pl.pallas_call(
        first_kernel,
        in_specs=[VMEM] * 2,
        out_specs=[VMEM] * 2,
        out_shape=[jax.ShapeDtypeStruct((rows, width), F32), jax.ShapeDtypeStruct((8, width), F32)],
        scratch_shapes=[pltpu.VMEM((rows - 2 * H, padded), BF16)] * 2,
        compiler_params=params(40),
        cost_estimate=pl.CostEstimate(flops=6 * 10**9, bytes_accessed=3 * 10**7, transcendentals=0),
        name="first_blur",
    )(pattern, first_taps)

    edge, send = pl.pallas_call(
        edge_kernel,
        in_specs=[VMEM] * 6,
        out_specs=[VMEM] * 2,
        out_shape=[jax.ShapeDtypeStruct((4 * H, width), F32), jax.ShapeDtypeStruct((count, LANES), F32)],
        compiler_params=params(40),
        name="edge_blur",
    )(for_odd, for_even, from_odd, from_even, sums, first_taps)

    gathered = lax.all_to_all(send.reshape(count, 1, LANES), AXES, 0, 0, tiled=True).reshape(count, LANES)

    cols = np.arange(cells, dtype=np.float64)
    across = back_weight(cols[:, None] - cols[None, :], fog_sigma)
    mix = np.zeros((LANES, 3 * LANES))
    for half in range(2):
        mine = slice(half * cells, (half + 1) * cells)
        other = slice((1 - half) * cells, (2 - half) * cells)
        mix[mine, mine] = across
        where = LANES if half == 1 else 2 * LANES
        mix[mine, where + other.start : where + other.stop] = across
    strips = np.arange(count, dtype=np.float64)
    gap = 2.0 * (strips[None, :] - strips[:, None])
    down = np.concatenate([back_weight(gap + shift, fog_sigma) for shift in (0.0, 1.0, -1.0)], axis=1)
    constants = [jnp.asarray(m) for m in two_terms(mix) + two_terms(down)]

    big = jnp.asarray(row_taps(wide, 1.0))
    small = jnp.asarray(row_taps(rows % wide, 1.0))
    return pl.pallas_call(
        second_kernel,
        in_specs=[VMEM] * 11,
        out_specs=[HBM] * 2,
        out_shape=[jax.ShapeDtypeStruct((rows, width), F32)] * 2,
        scratch_shapes=[pltpu.VMEM((rows, width), F32)] * 2
        + [pltpu.VMEM((rows, padded), BF16)] * 2
        + [pltpu.VMEM((8, width), F32)]
        + [pltpu.VMEM((count, LANES), F32)] * 2
        + [pltpu.SemaphoreType.DMA((cells,))] * 2,
        compiler_params=params(44),
        cost_estimate=pl.CostEstimate(flops=8 * 10**9, bytes_accessed=3 * 10**7, transcendentals=0),
        name="second_blur",
    )(now, edge, gathered, *constants, big, small, taps_high, taps_low)


def solution(mesh):
    return jax.shard_map(
        local,
        mesh=mesh,
        in_specs=(P(AXES, None),),
        out_specs=(P(AXES, None), P(AXES, None)),
        check_vma=False,
    )
```

```python
import functools
import math

import jax
import jax.numpy as jnp
import ml_dtypes
import numpy as np
from jax import lax
from jax.experimental import pallas as pl
from jax.experimental.pallas import tpu as pltpu
from jax.sharding import PartitionSpec as P

POOL = 256
H = 16
ETA_BACK = 0.75
SIGMA_BACK = 6.0
TOTAL = 1.0 + ETA_BACK
BACK_SHARE = ETA_BACK / TOTAL
AXES = ("band", "strip")
F32 = jnp.float32
BF16 = jnp.bfloat16
LANES = 128


def fine_taps(diff):
    spread = H / 3.0
    steps = np.arange(-H, H + 1, dtype=np.float64)
    total = np.exp(-steps * steps / (2.0 * spread * spread)).sum()
    weight = np.exp(-diff * diff / (2.0 * spread * spread)) / total
    return np.where(np.abs(diff) <= H, weight, 0.0)


def back_weight(diff, fog_sigma):
    near = np.exp(-diff * diff / (2.0 * SIGMA_BACK * SIGMA_BACK)) / (SIGMA_BACK * math.sqrt(2.0 * math.pi))
    far = np.exp(-diff * diff / (2.0 * fog_sigma * fog_sigma)) / (fog_sigma * math.sqrt(2.0 * math.pi))
    return 0.5 * near + 0.5 * far


def two_terms(matrix):
    high = matrix.astype(ml_dtypes.bfloat16)
    low = (matrix - high.astype(np.float64)).astype(ml_dtypes.bfloat16)
    return high, low


def row_taps(count, scale):
    out_rows = np.arange(count, dtype=np.float64)[:, None]
    in_rows = np.arange(count + 2 * H, dtype=np.float64)[None, :]
    return np.concatenate(two_terms(scale * fine_taps(in_rows - H - out_rows)), axis=0)


def column_taps(scale):
    ins = np.arange(POOL + 2 * LANES, dtype=np.float64)[:, None] - LANES
    outs = np.arange(POOL, dtype=np.float64)[None, :]
    return two_terms(scale * fine_taps(ins - outs))


def split(value):
    high = value.astype(BF16)
    low = (value - high.astype(F32)).astype(BF16)
    return high, low


def dot(a, b):
    return jnp.dot(a, b, preferred_element_type=F32)


def blur_down(taps, rows):
    both = dot(taps, rows)
    half = both.shape[0] // 2
    return both[:half] + both[half:]


def blur_down3(taps, high, low):
    half = taps.shape[0] // 2
    both = dot(taps, high)
    return both[:half] + both[half:] + dot(taps[:half], low)


def blur_across(high, low, taps_high, taps_low):
    return dot(high, taps_high) + dot(high, taps_low) + dot(low, taps_high)


def clear_rims(ref):
    zeros = jnp.zeros((ref.shape[0], LANES), BF16)
    ref[:, :LANES] = zeros
    ref[:, ref.shape[1] - LANES :] = zeros


def pixels(pattern):
    kind = pattern.astype(F32)
    return kind, jnp.where(pattern == 2, 7.0, 5.0 * kind)


LIFT = 1.05
MIDDLE = 1.85


def column_sums(value):
    return jnp.sum(value, axis=0, keepdims=True)


def windows(first, last, wide):
    return [(at, min(at + wide, last)) for at in range(first, last, wide)]


def rims_kernel(top_ref, bottom_ref, odd_ref, even_ref):
    even = lax.rem(lax.axis_index(AXES), 2) == 0
    odd_ref[...] = jnp.where(even, top_ref[...], bottom_ref[...])
    even_ref[...] = jnp.where(even, bottom_ref[...], top_ref[...])


def cut(packed_ref):
    column = POOL + 2 * LANES
    tall = 2 * (POOL - 2 * H)
    at = 2 * column + tall
    return packed_ref[:column], packed_ref[column : 2 * column], packed_ref[2 * column : at], packed_ref[at : at + 4 * H, : 4 * H]


def first_kernel(pattern_ref, taps_ref, out_ref, sums_ref, rh, rl):
    wh, wl, big, small = cut(taps_ref)
    rows, width = pattern_ref.shape
    cells = width // POOL
    clear_rims(rh)
    clear_rims(rl)
    parts = windows(H, rows - H, big.shape[1] - 2 * H)
    zeros = jnp.zeros((H, width), F32)
    out_ref[:H] = zeros
    out_ref[rows - H :] = zeros

    def cell(t):
        return slice(POOL * t, POOL * (t + 1))

    def down(t):
        here = slice(POOL * t + LANES, POOL * (t + 1) + LANES)
        _, level = pixels(pattern_ref[:, cell(t)])
        x = level.astype(BF16)
        for first, last in parts:
            taps = big if last - first + 2 * H == big.shape[1] else small
            part = blur_down(taps, x[first - H : last + H])
            rh[first - H : last - H, here], rl[first - H : last - H, here] = split(part)

    def across(t):
        window = slice(POOL * t, POOL * (t + 1) + 2 * LANES)
        forward = blur_across(rh[:, window], rl[:, window], wh, wl)
        kind, level = pixels(pattern_ref[:, cell(t)])
        now = jnp.maximum(1.5 * kind[H : rows - H] - forward, 0.0)
        out_ref[H : rows - H, cell(t)] = now
        sums = [column_sums(now[: POOL - H]), column_sums(now[POOL - H :])]
        sums += [column_sums(value[first : first + POOL]) for value in (level, kind) for first in (0, POOL)]
        sums_ref[:, cell(t)] = jnp.concatenate(sums + [jnp.zeros((2, POOL), F32)], axis=0)

    for t in range(cells + 1):
        if t < cells:
            down(t)
        if t > 0:
            across(t - 1)


def edge_kernel(for_odd_ref, for_even_ref, from_odd_ref, from_even_ref, sums_ref, taps_ref, edge_ref, send_ref):
    count = lax.axis_size(AXES)
    me = lax.axis_index(AXES)
    width = edge_ref.shape[1]
    wh, wl, _, taps = cut(taps_ref)
    cells = width // POOL
    even = lax.rem(me, 2) == 0
    top = jnp.where(even, for_odd_ref[...], for_even_ref[...])
    bottom = jnp.where(even, for_even_ref[...], for_odd_ref[...])
    above = jnp.where(even, from_odd_ref[...], from_even_ref[...])
    below = jnp.where(even, from_even_ref[...], from_odd_ref[...])
    above = jnp.where(me > 0, above, 0)
    below = jnp.where(me < count - 1, below, 0)
    upper = jnp.concatenate([above, top], axis=0)
    lower = jnp.concatenate([bottom, below], axis=0)
    blurred = [blur_down(taps, pixels(p)[1].astype(BF16)) for p in (upper, lower)]
    rim = jnp.zeros((4 * H, LANES), BF16)
    wide = [jnp.concatenate([rim, part, rim], axis=1) for part in split(jnp.concatenate(blurred, axis=0))]
    stacked = [
        jnp.concatenate([w[:, POOL * j : POOL * (j + 1) + 2 * LANES] for j in range(cells)], axis=0) for w in wide
    ]
    forward = blur_across(stacked[0], stacked[1], wh, wl)
    kind = jnp.concatenate([upper[H : 3 * H], lower[H : 3 * H]], axis=0).astype(F32)
    row = lax.broadcasted_iota(jnp.int32, (8, POOL), 0)
    place = lax.broadcasted_iota(jnp.int32, (8, LANES), 0)
    lane = lax.broadcasted_iota(jnp.int32, (8, LANES), 1)
    spread = jnp.zeros((8, LANES), F32)
    for j in range(cells):
        here = slice(POOL * j, POOL * (j + 1))
        now = jnp.maximum(1.5 * kind[:, here] - forward[4 * H * j : 4 * H * (j + 1)], 0.0)
        edge_ref[:, here] = now
        top, bottom = column_sums(now[H : 2 * H]), column_sums(now[2 * H : 3 * H])
        sums = sums_ref[:, here] + jnp.where(row == 0, top, jnp.where(row == 1, bottom, 0.0))
        total = jnp.sum(sums, axis=1, keepdims=True)
        value, fifths, classes = total[0:2], total[2:4], total[4:6]
        second = (5.0 * classes - fifths) * (1.0 / 3.0)
        total = jnp.concatenate([value - LIFT * second, 0.2 * fifths, classes - second, jnp.zeros((2, 1), F32)], axis=0)
        spread = spread + jnp.where(lane == place * cells + j, total, 0.0)
    line = column_sums(spread) * (1.0 / (POOL * POOL))
    send_ref[...] = jnp.broadcast_to(line, send_ref.shape)


def product(a, b):
    return dot(a[0], b[0]) + dot(a[1], b[0]) + dot(a[0], b[1])


def find_back(me, all_ref, mix, kernel, up_ref, b1_ref, b2_ref):
    count = all_ref.shape[0]
    cells = up_ref.shape[1] // POOL
    pair = 2 * cells
    adjusted = all_ref[...]
    coarse = pltpu.roll(adjusted, LANES - pair, 1)
    full = pltpu.roll(adjusted, LANES - 2 * pair, 1)

    def scatter(value):
        three = product(split(value), mix)
        return product(kernel, split(jnp.concatenate([three[:, LANES * i : LANES * (i + 1)] for i in range(3)], axis=0)))

    b1 = scatter(coarse)
    b1_ref[...] = b1
    b2_ref[...] = scatter(adjusted - BACK_SHARE * b1 * full)
    before = b1_ref[pl.ds(jnp.maximum(me - 1, 0), 1), :]
    here = b1_ref[pl.ds(me, 1), :]
    after = b1_ref[pl.ds(jnp.minimum(me + 1, count - 1), 1), :]
    own = b2_ref[pl.ds(me, 1), :]
    for at, (value, half) in enumerate(((before, 1), (here, 0), (here, 1), (after, 0), (own, 0), (own, 1))):
        value = BACK_SHARE * value
        for j in range(cells):
            lane = half * cells + j
            up_ref[at : at + 1, POOL * j : POOL * (j + 1)] = jnp.broadcast_to(value[:, lane : lane + 1], (1, POOL))


def second_kernel(
    now_ref, edge_ref, all_ref, mixh_ref, mixl_ref, kerh_ref, kerl_ref, big_ref, small_ref, wh_ref, wl_ref,
    dose_hbm, exposure_hbm,
    dose_ref, exposure_ref, rh, rl, up_ref, b1_ref, b2_ref, dose_sem, exposure_sem,
):
    rows, width = now_ref.shape
    cells = width // POOL
    big = big_ref.shape[1]
    wide = big - 2 * H

    def cell(t):
        return slice(POOL * t, POOL * (t + 1))

    parts = windows(0, rows, wide)
    stores = [
        [pltpu.make_async_copy(ref.at[a:b], hbm.at[a:b], sem.at[i]) for i, (a, b) in enumerate(parts)]
        for ref, hbm, sem in ((dose_ref, dose_hbm, dose_sem), (exposure_ref, exposure_hbm, exposure_sem))
    ]
    clear_rims(rh)
    clear_rims(rl)
    find_back(
        lax.axis_index(AXES), all_ref, (mixh_ref[...], mixl_ref[...]), (kerh_ref[...], kerl_ref[...]), up_ref, b1_ref, b2_ref
    )

    runs = [
        (-H, 0, edge_ref, 0, 0),
        (0, H, edge_ref, H, 1),
        (H, POOL, now_ref, H, 1),
        (POOL, rows - H, now_ref, POOL, 2),
        (rows - H, rows, edge_ref, 2 * H, 2),
        (rows, rows + H, edge_ref, 3 * H, 3),
    ]

    def dose_rows(first, last, t):
        doses = []
        for start, stop, ref, at, line in runs:
            a, b = max(start, first), min(stop, last)
            if a >= b:
                continue
            value = ref[at + a - start : at + b - start, cell(t)]
            second = value > MIDDLE
            dose = value - up_ref[line : line + 1, cell(t)]
            dose = jnp.maximum(jnp.where(second, dose - LIFT, dose), 0.0)
            doses.append(dose)
            low, high = max(a, first + H), min(b, last - H)
            if low < high:
                base = jnp.where(dose > 0, dose + jnp.where(second, 0.55, 0.5), 0.0)
                dose_ref[low:high, cell(t)] = base[low - a : high - a]
        return jnp.concatenate(doses, axis=0)

    def across(first, last, ts):
        spans = [slice(POOL * t, POOL * (t + 1) + 2 * LANES) for t in ts]
        high, low = (jnp.concatenate([ref[first:last, span] for span in spans], axis=0) for ref in (rh, rl))
        forward = blur_across(high, low, wh_ref[...], wl_ref[...])
        for k, t in enumerate(ts):
            here = cell(t)
            for half in range(rows // POOL):
                a, b = max(first, POOL * half), min(last, POOL * (half + 1))
                if a >= b:
                    continue
                at = k * (last - first) + a - first
                exposure = forward[at : at + b - a] + up_ref[4 + half : 5 + half, here]
                base = dose_ref[a:b, here]
                exposure_ref[a:b, here] = exposure
                dose_ref[a:b, here] = jnp.where(base > 0, base - exposure, 0.0)

    for i, (first, last) in enumerate(parts):
        full = last - first == wide
        taps = big_ref[...] if full else small_ref[...]
        for t in range(cells):
            here = slice(POOL * t + LANES, POOL * (t + 1) + LANES)
            part = blur_down3(taps, *split(dose_rows(first - H, last + H, t)))
            rh[first:last, here], rl[first:last, here] = split(part)
            if full and t > 0:
                across(first, last, [t - 1])
        across(first, last, [cells - 1] if full else list(range(cells)))
        for group in stores:
            group[i].start()
    for group in stores:
        for store in group:
            store.wait()


VMEM = pl.BlockSpec(memory_space=pltpu.VMEM)
HBM = pl.BlockSpec(memory_space=pltpu.HBM)


def local(pattern):
    rows, width = pattern.shape
    cells = width // POOL
    coarse_rows = rows // POOL
    count = lax.axis_size(AXES)
    fog_sigma = coarse_rows * count / 4.0
    wide = POOL - 2 * H
    padded = width + 2 * LANES
    def params(mebibytes):
        return pltpu.CompilerParams(vmem_limit_bytes=mebibytes * 2**20)

    odd_pairs = [(i, i if i in (0, count - 1) else ((i + 1) ^ 1) - 1) for i in range(count)]
    even_pairs = [(i, i ^ 1) for i in range(count)]
    strip = (2 * H, width)
    last_strip = rows // (2 * H) - 1
    for_odd, for_even = pl.pallas_call(
        rims_kernel,
        grid=(1,),
        in_specs=[pl.BlockSpec(strip, lambda i: (0, 0)), pl.BlockSpec(strip, lambda i: (last_strip, 0))],
        out_specs=[VMEM] * 2,
        out_shape=[jax.ShapeDtypeStruct(strip, pattern.dtype)] * 2,
        compiler_params=params(50),
        name="rims",
    )(pattern, pattern)
    from_odd = lax.ppermute(for_odd, AXES, odd_pairs)
    from_even = lax.ppermute(for_even, AXES, even_pairs)

    taps_high, taps_low = (jnp.asarray(m) for m in column_taps(1.0 / TOTAL))

    assert (rows - 2 * H) % wide in (0, 2 * H)
    short = row_taps(2 * H, 0.2)
    short = np.concatenate([short, np.zeros((short.shape[0], POOL - short.shape[1]), short.dtype)], axis=1)
    first_taps = jnp.asarray(np.concatenate([*column_taps(1.0 / TOTAL), row_taps(wide, 0.2), short], axis=0))
    now, sums = pl.pallas_call(
        first_kernel,
        in_specs=[VMEM] * 2,
        out_specs=[VMEM] * 2,
        out_shape=[jax.ShapeDtypeStruct((rows, width), F32), jax.ShapeDtypeStruct((8, width), F32)],
        scratch_shapes=[pltpu.VMEM((rows - 2 * H, padded), BF16)] * 2,
        compiler_params=params(40),
        cost_estimate=pl.CostEstimate(flops=6 * 10**9, bytes_accessed=3 * 10**7, transcendentals=0),
        name="first_blur",
    )(pattern, first_taps)

    edge, send = pl.pallas_call(
        edge_kernel,
        in_specs=[VMEM] * 6,
        out_specs=[VMEM] * 2,
        out_shape=[jax.ShapeDtypeStruct((4 * H, width), F32), jax.ShapeDtypeStruct((count, LANES), F32)],
        compiler_params=params(40),
        name="edge_blur",
    )(for_odd, for_even, from_odd, from_even, sums, first_taps)

    gathered = lax.all_to_all(send.reshape(count, 1, LANES), AXES, 0, 0, tiled=True).reshape(count, LANES)

    cols = np.arange(cells, dtype=np.float64)
    across = back_weight(cols[:, None] - cols[None, :], fog_sigma)
    mix = np.zeros((LANES, 3 * LANES))
    for half in range(2):
        mine = slice(half * cells, (half + 1) * cells)
        other = slice((1 - half) * cells, (2 - half) * cells)
        mix[mine, mine] = across
        where = LANES if half == 1 else 2 * LANES
        mix[mine, where + other.start : where + other.stop] = across
    strips = np.arange(count, dtype=np.float64)
    gap = 2.0 * (strips[None, :] - strips[:, None])
    down = np.concatenate([back_weight(gap + shift, fog_sigma) for shift in (0.0, 1.0, -1.0)], axis=1)
    constants = [jnp.asarray(m) for m in two_terms(mix) + two_terms(down)]

    big = jnp.asarray(row_taps(wide, 1.0))
    small = jnp.asarray(row_taps(rows % wide, 1.0))
    return pl.pallas_call(
        second_kernel,
        in_specs=[VMEM] * 11,
        out_specs=[HBM] * 2,
        out_shape=[jax.ShapeDtypeStruct((rows, width), F32)] * 2,
        scratch_shapes=[pltpu.VMEM((rows, width), F32)] * 2
        + [pltpu.VMEM((rows, padded), BF16)] * 2
        + [pltpu.VMEM((8, width), F32)]
        + [pltpu.VMEM((count, LANES), F32)] * 2
        + [pltpu.SemaphoreType.DMA((cells,))] * 2,
        compiler_params=params(44),
        cost_estimate=pl.CostEstimate(flops=8 * 10**9, bytes_accessed=3 * 10**7, transcendentals=0),
        name="second_blur",
    )(now, edge, gathered, *constants, big, small, taps_high, taps_low)


def solution(mesh):
    return jax.shard_map(
        local,
        mesh=mesh,
        in_specs=(P(AXES, None),),
        out_specs=(P(AXES, None), P(AXES, None)),
        check_vma=False,
    )
```

```python
import functools
import math

import jax
import jax.numpy as jnp
import ml_dtypes
import numpy as np
from jax import lax
from jax.experimental import pallas as pl
from jax.experimental.pallas import tpu as pltpu
from jax.sharding import PartitionSpec as P

POOL = 256
H = 16
ETA_BACK = 0.75
SIGMA_BACK = 6.0
TOTAL = 1.0 + ETA_BACK
BACK_SHARE = ETA_BACK / TOTAL
AXES = ("band", "strip")
F32 = jnp.float32
BF16 = jnp.bfloat16
LANES = 128


def fine_taps(diff):
    spread = H / 3.0
    steps = np.arange(-H, H + 1, dtype=np.float64)
    total = np.exp(-steps * steps / (2.0 * spread * spread)).sum()
    weight = np.exp(-diff * diff / (2.0 * spread * spread)) / total
    return np.where(np.abs(diff) <= H, weight, 0.0)


def back_weight(diff, fog_sigma):
    near = np.exp(-diff * diff / (2.0 * SIGMA_BACK * SIGMA_BACK)) / (SIGMA_BACK * math.sqrt(2.0 * math.pi))
    far = np.exp(-diff * diff / (2.0 * fog_sigma * fog_sigma)) / (fog_sigma * math.sqrt(2.0 * math.pi))
    return 0.5 * near + 0.5 * far


def two_terms(matrix):
    high = matrix.astype(ml_dtypes.bfloat16)
    low = (matrix - high.astype(np.float64)).astype(ml_dtypes.bfloat16)
    return high, low


def row_taps(count, scale):
    out_rows = np.arange(count, dtype=np.float64)[:, None]
    in_rows = np.arange(count + 2 * H, dtype=np.float64)[None, :]
    return np.concatenate(two_terms(scale * fine_taps(in_rows - H - out_rows)), axis=0)


def column_taps(scale):
    ins = np.arange(POOL + 2 * LANES, dtype=np.float64)[:, None] - LANES
    outs = np.arange(POOL, dtype=np.float64)[None, :]
    return two_terms(scale * fine_taps(ins - outs))


def split(value):
    high = value.astype(BF16)
    low = (value - high.astype(F32)).astype(BF16)
    return high, low


def dot(a, b):
    return jnp.dot(a, b, preferred_element_type=F32)


def blur_down(taps, rows):
    both = dot(taps, rows)
    half = both.shape[0] // 2
    return both[:half] + both[half:]


def blur_down3(taps, high, low):
    half = taps.shape[0] // 2
    both = dot(taps, high)
    return both[:half] + both[half:] + dot(taps[:half], low)


def blur_across(high, low, taps_high, taps_low):
    return dot(high, taps_high) + dot(high, taps_low) + dot(low, taps_high)


def clear_rims(ref):
    zeros = jnp.zeros((ref.shape[0], LANES), BF16)
    ref[:, :LANES] = zeros
    ref[:, ref.shape[1] - LANES :] = zeros


def pixels(pattern):
    kind = pattern.astype(F32)
    return kind, jnp.where(pattern == 2, 7.0, 5.0 * kind)


def first_update(kind, forward):
    second = kind > 1.5
    value = jnp.maximum(1.5 * kind - forward, 0.0)
    value = jnp.where(second, value - 1.05, value)
    return value, jnp.where(kind > 0.5, value + jnp.where(second, 0.55, 0.5), 0.0)


def column_sums(value):
    return jnp.sum(value, axis=0, keepdims=True)


def windows(first, last, wide):
    return [(at, min(at + wide, last)) for at in range(first, last, wide)]


def rims_kernel(top_ref, bottom_ref, odd_ref, even_ref):
    even = lax.rem(lax.axis_index(AXES), 2) == 0
    odd_ref[...] = jnp.where(even, top_ref[...], bottom_ref[...])
    even_ref[...] = jnp.where(even, bottom_ref[...], top_ref[...])


def cut(packed_ref):
    column = POOL + 2 * LANES
    tall = 2 * (POOL - 2 * H)
    at = 2 * column + tall
    return packed_ref[:column], packed_ref[column : 2 * column], packed_ref[2 * column : at], packed_ref[at : at + 4 * H, : 4 * H]


def first_kernel(pattern_ref, taps_ref, out_ref, base_ref, sums_ref, rh, rl):
    wh, wl, big, small = cut(taps_ref)
    rows, width = pattern_ref.shape
    cells = width // POOL
    clear_rims(rh)
    clear_rims(rl)
    parts = windows(H, rows - H, big.shape[1] - 2 * H)
    zeros = jnp.zeros((H, width), F32)
    for ref in (out_ref, base_ref):
        ref[:H] = zeros
        ref[rows - H :] = zeros

    def cell(t):
        return slice(POOL * t, POOL * (t + 1))

    def down(t):
        here = slice(POOL * t + LANES, POOL * (t + 1) + LANES)
        _, level = pixels(pattern_ref[:, cell(t)])
        x = level.astype(BF16)
        for first, last in parts:
            taps = big if last - first + 2 * H == big.shape[1] else small
            part = blur_down(taps, x[first - H : last + H])
            rh[first - H : last - H, here], rl[first - H : last - H, here] = split(part)

    def across(t):
        window = slice(POOL * t, POOL * (t + 1) + 2 * LANES)
        forward = blur_across(rh[:, window], rl[:, window], wh, wl)
        kind, level = pixels(pattern_ref[:, cell(t)])
        now, base = first_update(kind[H : rows - H], forward)
        out_ref[H : rows - H, cell(t)] = now
        base_ref[H : rows - H, cell(t)] = base
        sums = [column_sums(now[: POOL - H]), column_sums(now[POOL - H :])]
        sums += [column_sums(value[first : first + POOL]) for value in (level, kind) for first in (0, POOL)]
        sums_ref[:, cell(t)] = jnp.concatenate(sums + [jnp.zeros((2, POOL), F32)], axis=0)

    for t in range(cells + 1):
        if t < cells:
            down(t)
        if t > 0:
            across(t - 1)


def edge_kernel(for_odd_ref, for_even_ref, from_odd_ref, from_even_ref, sums_ref, taps_ref, edge_ref, edge_base_ref, send_ref):
    count = lax.axis_size(AXES)
    me = lax.axis_index(AXES)
    width = edge_ref.shape[1]
    wh, wl, _, taps = cut(taps_ref)
    cells = width // POOL
    even = lax.rem(me, 2) == 0
    top = jnp.where(even, for_odd_ref[...], for_even_ref[...])
    bottom = jnp.where(even, for_even_ref[...], for_odd_ref[...])
    above = jnp.where(even, from_odd_ref[...], from_even_ref[...])
    below = jnp.where(even, from_even_ref[...], from_odd_ref[...])
    above = jnp.where(me > 0, above, 0)
    below = jnp.where(me < count - 1, below, 0)
    upper = jnp.concatenate([above, top], axis=0)
    lower = jnp.concatenate([bottom, below], axis=0)
    blurred = [blur_down(taps, pixels(p)[1].astype(BF16)) for p in (upper, lower)]
    rim = jnp.zeros((4 * H, LANES), BF16)
    wide = [jnp.concatenate([rim, part, rim], axis=1) for part in split(jnp.concatenate(blurred, axis=0))]
    stacked = [
        jnp.concatenate([w[:, POOL * j : POOL * (j + 1) + 2 * LANES] for j in range(cells)], axis=0) for w in wide
    ]
    forward = blur_across(stacked[0], stacked[1], wh, wl)
    kind = jnp.concatenate([upper[H : 3 * H], lower[H : 3 * H]], axis=0).astype(F32)
    row = lax.broadcasted_iota(jnp.int32, (8, POOL), 0)
    place = lax.broadcasted_iota(jnp.int32, (8, LANES), 0)
    lane = lax.broadcasted_iota(jnp.int32, (8, LANES), 1)
    spread = jnp.zeros((8, LANES), F32)
    for j in range(cells):
        here = slice(POOL * j, POOL * (j + 1))
        now, edge_base_ref[:, here] = first_update(kind[:, here], forward[4 * H * j : 4 * H * (j + 1)])
        edge_ref[:, here] = now
        top, bottom = column_sums(now[H : 2 * H]), column_sums(now[2 * H : 3 * H])
        sums = sums_ref[:, here] + jnp.where(row == 0, top, jnp.where(row == 1, bottom, 0.0))
        total = jnp.sum(sums, axis=1, keepdims=True)
        value, fifths, classes = total[0:2], total[2:4], total[4:6]
        second = (5.0 * classes - fifths) * (1.0 / 3.0)
        total = jnp.concatenate([value, 0.2 * fifths, classes - second, jnp.zeros((2, 1), F32)], axis=0)
        spread = spread + jnp.where(lane == place * cells + j, total, 0.0)
    line = column_sums(spread) * (1.0 / (POOL * POOL))
    send_ref[...] = jnp.broadcast_to(line, send_ref.shape)


def product(a, b):
    return dot(a[0], b[0]) + dot(a[1], b[0]) + dot(a[0], b[1])


def find_back(me, all_ref, mix, kernel, up_ref, b1_ref, b2_ref):
    count = all_ref.shape[0]
    cells = up_ref.shape[1] // POOL
    pair = 2 * cells
    adjusted = all_ref[...]
    coarse = pltpu.roll(adjusted, LANES - pair, 1)
    full = pltpu.roll(adjusted, LANES - 2 * pair, 1)

    def scatter(value):
        three = product(split(value), mix)
        return product(kernel, split(jnp.concatenate([three[:, LANES * i : LANES * (i + 1)] for i in range(3)], axis=0)))

    b1 = scatter(coarse)
    b1_ref[...] = b1
    b2_ref[...] = scatter(adjusted - BACK_SHARE * b1 * full)
    before = b1_ref[pl.ds(jnp.maximum(me - 1, 0), 1), :]
    here = b1_ref[pl.ds(me, 1), :]
    after = b1_ref[pl.ds(jnp.minimum(me + 1, count - 1), 1), :]
    own = b2_ref[pl.ds(me, 1), :]
    for at, (value, half) in enumerate(((before, 1), (here, 0), (here, 1), (after, 0), (own, 0), (own, 1))):
        value = BACK_SHARE * value
        for j in range(cells):
            lane = half * cells + j
            up_ref[at : at + 1, POOL * j : POOL * (j + 1)] = jnp.broadcast_to(value[:, lane : lane + 1], (1, POOL))


def second_kernel(
    now_ref, base_ref, edge_ref, edge_base_ref, all_ref, mixh_ref, mixl_ref, kerh_ref, kerl_ref, big_ref, small_ref, wh_ref, wl_ref,
    dose_hbm, exposure_hbm,
    dose_ref, exposure_ref, rh, rl, up_ref, b1_ref, b2_ref, dose_sem, exposure_sem,
):
    rows, width = now_ref.shape
    cells = width // POOL
    big = big_ref.shape[1]
    wide = big - 2 * H

    def cell(t):
        return slice(POOL * t, POOL * (t + 1))

    parts = [(0, 224), (224, 416), (416, 512)]
    stores = [
        [pltpu.make_async_copy(ref.at[a:b], hbm.at[a:b], sem.at[i]) for i, (a, b) in enumerate(parts)]
        for ref, hbm, sem in ((dose_ref, dose_hbm, dose_sem), (exposure_ref, exposure_hbm, exposure_sem))
    ]
    clear_rims(rh)
    clear_rims(rl)
    find_back(
        lax.axis_index(AXES), all_ref, (mixh_ref[...], mixl_ref[...]), (kerh_ref[...], kerl_ref[...]), up_ref, b1_ref, b2_ref
    )

    runs = [
        (-H, 0, edge_ref, 0, 0),
        (0, H, edge_ref, H, 1),
        (H, POOL, now_ref, H, 1),
        (POOL, rows - H, now_ref, POOL, 2),
        (rows - H, rows, edge_ref, 2 * H, 2),
        (rows, rows + H, edge_ref, 3 * H, 3),
    ]

    def dose_rows(first, last, t):
        doses = []
        for start, stop, ref, at, line in runs:
            a, b = max(start, first), min(stop, last)
            if a >= b:
                continue
            value = ref[at + a - start : at + b - start, cell(t)]
            doses.append(jnp.maximum(value - up_ref[line : line + 1, cell(t)], 0.0))
        return jnp.concatenate(doses, axis=0)

    own = [
        (0, H, edge_base_ref, H, 0),
        (H, POOL, base_ref, H, 0),
        (POOL, rows - H, base_ref, POOL, 1),
        (rows - H, rows, edge_base_ref, 2 * H, 1),
    ]

    def across(first, last, ts):
        spans = [slice(POOL * t, POOL * (t + 1) + 2 * LANES) for t in ts]
        high, low = (jnp.concatenate([ref[first:last, span] for span in spans], axis=0) for ref in (rh, rl))
        forward = blur_across(high, low, wh_ref[...], wl_ref[...])
        for k, t in enumerate(ts):
            here = cell(t)
            for start, stop, ref, from_row, half in own:
                a, b = max(first, start), min(last, stop)
                if a >= b:
                    continue
                at = k * (last - first) + a - first
                part = forward[at : at + b - a]
                second = up_ref[4 + half : 5 + half, here]
                base = ref[from_row + a - start : from_row + b - start, here]
                exposure_ref[a:b, here] = part + second
                dose_ref[a:b, here] = jnp.where(base > 0, base - (up_ref[1 + half : 2 + half, here] + second) - part, 0.0)

    for i, (first, last) in enumerate(parts):
        n = last - first
        full = n > 96
        taps = big_ref[...] if n == wide else jnp.concatenate([big_ref[:n, : n + 2 * H], big_ref[wide : wide + n, : n + 2 * H]], axis=0)
        for t in range(cells):
            here = slice(POOL * t + LANES, POOL * (t + 1) + LANES)
            part = blur_down3(taps, *split(dose_rows(first - H, last + H, t)))
            rh[first:last, here], rl[first:last, here] = split(part)
            if full and t > 0:
                across(first, last, [t - 1])
        across(first, last, [cells - 1] if full else list(range(cells)))
        for group in stores:
            group[i].start()
    for group in stores:
        for store in group:
            store.wait()


VMEM = pl.BlockSpec(memory_space=pltpu.VMEM)
HBM = pl.BlockSpec(memory_space=pltpu.HBM)


def local(pattern):
    rows, width = pattern.shape
    cells = width // POOL
    coarse_rows = rows // POOL
    count = lax.axis_size(AXES)
    fog_sigma = coarse_rows * count / 4.0
    wide = POOL - 2 * H
    padded = width + 2 * LANES
    def params(mebibytes):
        return pltpu.CompilerParams(vmem_limit_bytes=mebibytes * 2**20)

    odd_pairs = [(i, i if i in (0, count - 1) else ((i + 1) ^ 1) - 1) for i in range(count)]
    even_pairs = [(i, i ^ 1) for i in range(count)]
    strip = (2 * H, width)
    last_strip = rows // (2 * H) - 1
    for_odd, for_even = pl.pallas_call(
        rims_kernel,
        grid=(1,),
        in_specs=[pl.BlockSpec(strip, lambda i: (0, 0)), pl.BlockSpec(strip, lambda i: (last_strip, 0))],
        out_specs=[VMEM] * 2,
        out_shape=[jax.ShapeDtypeStruct(strip, pattern.dtype)] * 2,
        compiler_params=params(50),
        name="rims",
    )(pattern, pattern)
    from_odd = lax.ppermute(for_odd, AXES, odd_pairs)
    from_even = lax.ppermute(for_even, AXES, even_pairs)

    taps_high, taps_low = (jnp.asarray(m) for m in column_taps(1.0 / TOTAL))

    assert (rows - 2 * H) % wide in (0, 2 * H)
    short = row_taps(2 * H, 0.2)
    short = np.concatenate([short, np.zeros((short.shape[0], POOL - short.shape[1]), short.dtype)], axis=1)
    first_taps = jnp.asarray(np.concatenate([*column_taps(1.0 / TOTAL), row_taps(wide, 0.2), short], axis=0))
    now, base, sums = pl.pallas_call(
        first_kernel,
        in_specs=[VMEM] * 2,
        out_specs=[VMEM] * 3,
        out_shape=[jax.ShapeDtypeStruct((rows, width), F32)] * 2 + [jax.ShapeDtypeStruct((8, width), F32)],
        scratch_shapes=[pltpu.VMEM((rows - 2 * H, padded), BF16)] * 2,
        compiler_params=params(28),
        cost_estimate=pl.CostEstimate(flops=6 * 10**9, bytes_accessed=3 * 10**7, transcendentals=0),
        name="first_blur",
    )(pattern, first_taps)

    edge, edge_base, send = pl.pallas_call(
        edge_kernel,
        in_specs=[VMEM] * 6,
        out_specs=[VMEM] * 3,
        out_shape=[jax.ShapeDtypeStruct((4 * H, width), F32)] * 2 + [jax.ShapeDtypeStruct((count, LANES), F32)],
        compiler_params=params(28),
        name="edge_blur",
    )(for_odd, for_even, from_odd, from_even, sums, first_taps)

    gathered = lax.all_to_all(send.reshape(count, 1, LANES), AXES, 0, 0, tiled=True).reshape(count, LANES)

    cols = np.arange(cells, dtype=np.float64)
    across = back_weight(cols[:, None] - cols[None, :], fog_sigma)
    mix = np.zeros((LANES, 3 * LANES))
    for half in range(2):
        mine = slice(half * cells, (half + 1) * cells)
        other = slice((1 - half) * cells, (2 - half) * cells)
        mix[mine, mine] = across
        where = LANES if half == 1 else 2 * LANES
        mix[mine, where + other.start : where + other.stop] = across
    strips = np.arange(count, dtype=np.float64)
    gap = 2.0 * (strips[None, :] - strips[:, None])
    down = np.concatenate([back_weight(gap + shift, fog_sigma) for shift in (0.0, 1.0, -1.0)], axis=1)
    constants = [jnp.asarray(m) for m in two_terms(mix) + two_terms(down)]

    big = jnp.asarray(row_taps(wide, 1.0))
    small = jnp.asarray(row_taps(rows % wide, 1.0))
    return pl.pallas_call(
        second_kernel,
        in_specs=[VMEM] * 13,
        out_specs=[HBM] * 2,
        out_shape=[jax.ShapeDtypeStruct((rows, width), F32)] * 2,
        scratch_shapes=[pltpu.VMEM((rows, width), F32)] * 2
        + [pltpu.VMEM((rows, padded), BF16)] * 2
        + [pltpu.VMEM((8, width), F32)]
        + [pltpu.VMEM((count, LANES), F32)] * 2
        + [pltpu.SemaphoreType.DMA((cells,))] * 2,
        compiler_params=params(36),
        cost_estimate=pl.CostEstimate(flops=8 * 10**9, bytes_accessed=3 * 10**7, transcendentals=0),
        name="second_blur",
    )(now, base, edge, edge_base, gathered, *constants, big, small, taps_high, taps_low)


def solution(mesh):
    return jax.shard_map(
        local,
        mesh=mesh,
        in_specs=(P(AXES, None),),
        out_specs=(P(AXES, None), P(AXES, None)),
        check_vma=False,
    )
```

```python
import functools
import math

import jax
import jax.numpy as jnp
import ml_dtypes
import numpy as np
from jax import lax
from jax.experimental import pallas as pl
from jax.experimental.pallas import tpu as pltpu
from jax.sharding import PartitionSpec as P

POOL = 256
H = 16
ETA_BACK = 0.75
SIGMA_BACK = 6.0
TOTAL = 1.0 + ETA_BACK
BACK_SHARE = ETA_BACK / TOTAL
AXES = ("band", "strip")
F32 = jnp.float32
BF16 = jnp.bfloat16
LANES = 128


def fine_taps(diff):
    spread = H / 3.0
    steps = np.arange(-H, H + 1, dtype=np.float64)
    total = np.exp(-steps * steps / (2.0 * spread * spread)).sum()
    weight = np.exp(-diff * diff / (2.0 * spread * spread)) / total
    return np.where(np.abs(diff) <= H, weight, 0.0)


def back_weight(diff, fog_sigma):
    near = np.exp(-diff * diff / (2.0 * SIGMA_BACK * SIGMA_BACK)) / (SIGMA_BACK * math.sqrt(2.0 * math.pi))
    far = np.exp(-diff * diff / (2.0 * fog_sigma * fog_sigma)) / (fog_sigma * math.sqrt(2.0 * math.pi))
    return 0.5 * near + 0.5 * far


def two_terms(matrix):
    high = matrix.astype(ml_dtypes.bfloat16)
    low = (matrix - high.astype(np.float64)).astype(ml_dtypes.bfloat16)
    return high, low


def row_taps(count, scale):
    out_rows = np.arange(count, dtype=np.float64)[:, None]
    in_rows = np.arange(count + 2 * H, dtype=np.float64)[None, :]
    return np.concatenate(two_terms(scale * fine_taps(in_rows - H - out_rows)), axis=0)


def column_taps(scale):
    ins = np.arange(POOL + 2 * LANES, dtype=np.float64)[:, None] - LANES
    outs = np.arange(POOL, dtype=np.float64)[None, :]
    return two_terms(scale * fine_taps(ins - outs))


def split(value):
    high = value.astype(BF16)
    low = (value - high.astype(F32)).astype(BF16)
    return high, low


def dot(a, b):
    return jnp.dot(a, b, preferred_element_type=F32)


def blur_down(taps, rows):
    both = dot(taps, rows)
    half = both.shape[0] // 2
    return both[:half] + both[half:]


def blur_down3(taps, high, low):
    half = taps.shape[0] // 2
    both = dot(taps, high)
    return both[:half] + both[half:] + dot(taps[:half], low)


def blur_across(high, low, taps_high, taps_low):
    return dot(high, taps_high) + dot(high, taps_low) + dot(low, taps_high)


def clear_rims(ref):
    zeros = jnp.zeros((ref.shape[0], LANES), BF16)
    ref[:, :LANES] = zeros
    ref[:, ref.shape[1] - LANES :] = zeros


def pixels(pattern):
    kind = pattern.astype(F32)
    return kind, jnp.where(pattern == 2, 7.0, 5.0 * kind)


def first_update(kind, forward):
    second = kind > 1.5
    value = jnp.maximum(1.5 * kind - forward, 0.0)
    value = jnp.where(second, value - 1.05, value)
    return value, jnp.where(kind > 0.5, value + jnp.where(second, 0.55, 0.5), 0.0)


def column_sums(value):
    return jnp.sum(value, axis=0, keepdims=True)


def windows(first, last, wide):
    return [(at, min(at + wide, last)) for at in range(first, last, wide)]


def rims_kernel(top_ref, bottom_ref, odd_ref, even_ref):
    even = lax.rem(lax.axis_index(AXES), 2) == 0
    odd_ref[...] = jnp.where(even, top_ref[...], bottom_ref[...])
    even_ref[...] = jnp.where(even, bottom_ref[...], top_ref[...])


def cut(packed_ref):
    column = POOL + 2 * LANES
    tall = 2 * (POOL - 2 * H)
    at = 2 * column + tall
    return packed_ref[:column], packed_ref[column : 2 * column], packed_ref[2 * column : at], packed_ref[at : at + 4 * H, : 4 * H]


def first_kernel(pattern_ref, taps_ref, out_ref, base_ref, sums_ref, rh, rl):
    wh, wl, big, small = cut(taps_ref)
    rows, width = pattern_ref.shape
    cells = width // POOL
    clear_rims(rh)
    clear_rims(rl)
    parts = windows(H, rows - H, big.shape[1] - 2 * H)
    zeros = jnp.zeros((H, width), F32)
    for ref in (out_ref, base_ref):
        ref[:H] = zeros
        ref[rows - H :] = zeros

    def cell(t):
        return slice(POOL * t, POOL * (t + 1))

    def down(t):
        here = slice(POOL * t + LANES, POOL * (t + 1) + LANES)
        _, level = pixels(pattern_ref[:, cell(t)])
        x = level.astype(BF16)
        for first, last in parts:
            taps = big if last - first + 2 * H == big.shape[1] else small
            part = blur_down(taps, x[first - H : last + H])
            rh[first - H : last - H, here], rl[first - H : last - H, here] = split(part)

    def across(t):
        window = slice(POOL * t, POOL * (t + 1) + 2 * LANES)
        forward = blur_across(rh[:, window], rl[:, window], wh, wl)
        kind, level = pixels(pattern_ref[:, cell(t)])
        now, base = first_update(kind[H : rows - H], forward)
        out_ref[H : rows - H, cell(t)] = now
        base_ref[H : rows - H, cell(t)] = base
        sums = [column_sums(now[: POOL - H]), column_sums(now[POOL - H :])]
        sums += [column_sums(value[first : first + POOL]) for value in (level, kind) for first in (0, POOL)]
        sums_ref[:, cell(t)] = jnp.concatenate(sums + [jnp.zeros((2, POOL), F32)], axis=0)

    for t in range(cells + 2):
        if t < cells:
            down(t)
        if t > 1:
            across(t - 2)


def edge_kernel(for_odd_ref, for_even_ref, from_odd_ref, from_even_ref, sums_ref, taps_ref, edge_ref, edge_base_ref, send_ref):
    count = lax.axis_size(AXES)
    me = lax.axis_index(AXES)
    width = edge_ref.shape[1]
    wh, wl, _, taps = cut(taps_ref)
    cells = width // POOL
    even = lax.rem(me, 2) == 0
    top = jnp.where(even, for_odd_ref[...], for_even_ref[...])
    bottom = jnp.where(even, for_even_ref[...], for_odd_ref[...])
    above = jnp.where(even, from_odd_ref[...], from_even_ref[...])
    below = jnp.where(even, from_even_ref[...], from_odd_ref[...])
    above = jnp.where(me > 0, above, 0)
    below = jnp.where(me < count - 1, below, 0)
    upper = jnp.concatenate([above, top], axis=0)
    lower = jnp.concatenate([bottom, below], axis=0)
    blurred = [blur_down(taps, pixels(p)[1].astype(BF16)) for p in (upper, lower)]
    rim = jnp.zeros((4 * H, LANES), BF16)
    wide = [jnp.concatenate([rim, part, rim], axis=1) for part in split(jnp.concatenate(blurred, axis=0))]
    stacked = [
        jnp.concatenate([w[:, POOL * j : POOL * (j + 1) + 2 * LANES] for j in range(cells)], axis=0) for w in wide
    ]
    forward = blur_across(stacked[0], stacked[1], wh, wl)
    kind = jnp.concatenate([upper[H : 3 * H], lower[H : 3 * H]], axis=0).astype(F32)
    row = lax.broadcasted_iota(jnp.int32, (8, POOL), 0)
    place = lax.broadcasted_iota(jnp.int32, (8, LANES), 0)
    lane = lax.broadcasted_iota(jnp.int32, (8, LANES), 1)
    spread = jnp.zeros((8, LANES), F32)
    for j in range(cells):
        here = slice(POOL * j, POOL * (j + 1))
        now, edge_base_ref[:, here] = first_update(kind[:, here], forward[4 * H * j : 4 * H * (j + 1)])
        edge_ref[:, here] = now
        top, bottom = column_sums(now[H : 2 * H]), column_sums(now[2 * H : 3 * H])
        sums = sums_ref[:, here] + jnp.where(row == 0, top, jnp.where(row == 1, bottom, 0.0))
        total = jnp.sum(sums, axis=1, keepdims=True)
        value, fifths, classes = total[0:2], total[2:4], total[4:6]
        second = (5.0 * classes - fifths) * (1.0 / 3.0)
        total = jnp.concatenate([value, 0.2 * fifths, classes - second, jnp.zeros((2, 1), F32)], axis=0)
        spread = spread + jnp.where(lane == place * cells + j, total, 0.0)
    line = column_sums(spread) * (1.0 / (POOL * POOL))
    send_ref[...] = jnp.broadcast_to(line, send_ref.shape)


def product(a, b):
    return dot(a[0], b[0]) + dot(a[1], b[0]) + dot(a[0], b[1])


def find_back(me, all_ref, mix, kernel, up_ref, b1_ref, b2_ref):
    count = all_ref.shape[0]
    cells = up_ref.shape[1] // POOL
    pair = 2 * cells
    adjusted = all_ref[...]
    coarse = pltpu.roll(adjusted, LANES - pair, 1)
    full = pltpu.roll(adjusted, LANES - 2 * pair, 1)

    def scatter(value):
        three = product(split(value), mix)
        return product(kernel, split(jnp.concatenate([three[:, LANES * i : LANES * (i + 1)] for i in range(3)], axis=0)))

    b1 = scatter(coarse)
    b1_ref[...] = b1
    b2_ref[...] = scatter(adjusted - BACK_SHARE * b1 * full)
    before = b1_ref[pl.ds(jnp.maximum(me - 1, 0), 1), :]
    here = b1_ref[pl.ds(me, 1), :]
    after = b1_ref[pl.ds(jnp.minimum(me + 1, count - 1), 1), :]
    own = b2_ref[pl.ds(me, 1), :]
    for at, (value, half) in enumerate(((before, 1), (here, 0), (here, 1), (after, 0), (own, 0), (own, 1))):
        value = BACK_SHARE * value
        for j in range(cells):
            lane = half * cells + j
            up_ref[at : at + 1, POOL * j : POOL * (j + 1)] = jnp.broadcast_to(value[:, lane : lane + 1], (1, POOL))


def second_kernel(
    now_ref, base_ref, edge_ref, edge_base_ref, all_ref, mixh_ref, mixl_ref, kerh_ref, kerl_ref, big_ref, small_ref, wh_ref, wl_ref,
    dose_hbm, exposure_hbm,
    dose_ref, exposure_ref, rh, rl, up_ref, b1_ref, b2_ref, dose_sem, exposure_sem,
):
    rows, width = now_ref.shape
    cells = width // POOL
    big = big_ref.shape[1]
    wide = big - 2 * H

    def cell(t):
        return slice(POOL * t, POOL * (t + 1))

    parts = [(0, 224), (224, 416), (416, 512)]
    stores = [
        [pltpu.make_async_copy(ref.at[a:b], hbm.at[a:b], sem.at[i]) for i, (a, b) in enumerate(parts)]
        for ref, hbm, sem in ((dose_ref, dose_hbm, dose_sem), (exposure_ref, exposure_hbm, exposure_sem))
    ]
    clear_rims(rh)
    clear_rims(rl)
    find_back(
        lax.axis_index(AXES), all_ref, (mixh_ref[...], mixl_ref[...]), (kerh_ref[...], kerl_ref[...]), up_ref, b1_ref, b2_ref
    )

    runs = [
        (-H, 0, edge_ref, 0, 0),
        (0, H, edge_ref, H, 1),
        (H, POOL, now_ref, H, 1),
        (POOL, rows - H, now_ref, POOL, 2),
        (rows - H, rows, edge_ref, 2 * H, 2),
        (rows, rows + H, edge_ref, 3 * H, 3),
    ]

    def dose_rows(first, last, t):
        doses = []
        for start, stop, ref, at, line in runs:
            a, b = max(start, first), min(stop, last)
            if a >= b:
                continue
            value = ref[at + a - start : at + b - start, cell(t)]
            doses.append(jnp.maximum(value - up_ref[line : line + 1, cell(t)], 0.0))
        return jnp.concatenate(doses, axis=0)

    own = [
        (0, H, edge_base_ref, H, 0),
        (H, POOL, base_ref, H, 0),
        (POOL, rows - H, base_ref, POOL, 1),
        (rows - H, rows, edge_base_ref, 2 * H, 1),
    ]

    def across(first, last, ts):
        spans = [slice(POOL * t, POOL * (t + 1) + 2 * LANES) for t in ts]
        high, low = (jnp.concatenate([ref[first:last, span] for span in spans], axis=0) for ref in (rh, rl))
        forward = blur_across(high, low, wh_ref[...], wl_ref[...])
        for k, t in enumerate(ts):
            here = cell(t)
            for start, stop, ref, from_row, half in own:
                a, b = max(first, start), min(last, stop)
                if a >= b:
                    continue
                at = k * (last - first) + a - first
                part = forward[at : at + b - a]
                second = up_ref[4 + half : 5 + half, here]
                base = ref[from_row + a - start : from_row + b - start, here]
                exposure_ref[a:b, here] = part + second
                dose_ref[a:b, here] = jnp.where(base > 0, base - (up_ref[1 + half : 2 + half, here] + second) - part, 0.0)

    for i, (first, last) in enumerate(parts):
        n = last - first
        full = n > 96
        taps = big_ref[...] if n == wide else jnp.concatenate([big_ref[:n, : n + 2 * H], big_ref[wide : wide + n, : n + 2 * H]], axis=0)
        for t in range(cells):
            here = slice(POOL * t + LANES, POOL * (t + 1) + LANES)
            part = blur_down3(taps, *split(dose_rows(first - H, last + H, t)))
            rh[first:last, here], rl[first:last, here] = split(part)
            if full and t > 1:
                across(first, last, [t - 2])
        for group in [[cells - 2], [cells - 1]] if full else [list(range(cells))]:
            across(first, last, group)
        for group in stores:
            group[i].start()
    for group in stores:
        for store in group:
            store.wait()


VMEM = pl.BlockSpec(memory_space=pltpu.VMEM)
HBM = pl.BlockSpec(memory_space=pltpu.HBM)


def local(pattern):
    rows, width = pattern.shape
    cells = width // POOL
    coarse_rows = rows // POOL
    count = lax.axis_size(AXES)
    fog_sigma = coarse_rows * count / 4.0
    wide = POOL - 2 * H
    padded = width + 2 * LANES
    def params(mebibytes):
        return pltpu.CompilerParams(vmem_limit_bytes=mebibytes * 2**20)

    odd_pairs = [(i, i if i in (0, count - 1) else ((i + 1) ^ 1) - 1) for i in range(count)]
    even_pairs = [(i, i ^ 1) for i in range(count)]
    strip = (2 * H, width)
    last_strip = rows // (2 * H) - 1
    for_odd, for_even = pl.pallas_call(
        rims_kernel,
        grid=(1,),
        in_specs=[pl.BlockSpec(strip, lambda i: (0, 0)), pl.BlockSpec(strip, lambda i: (last_strip, 0))],
        out_specs=[VMEM] * 2,
        out_shape=[jax.ShapeDtypeStruct(strip, pattern.dtype)] * 2,
        compiler_params=params(50),
        name="rims",
    )(pattern, pattern)
    from_odd = lax.ppermute(for_odd, AXES, odd_pairs)
    from_even = lax.ppermute(for_even, AXES, even_pairs)

    taps_high, taps_low = (jnp.asarray(m) for m in column_taps(1.0 / TOTAL))

    assert (rows - 2 * H) % wide in (0, 2 * H)
    short = row_taps(2 * H, 0.2)
    short = np.concatenate([short, np.zeros((short.shape[0], POOL - short.shape[1]), short.dtype)], axis=1)
    first_taps = jnp.asarray(np.concatenate([*column_taps(1.0 / TOTAL), row_taps(wide, 0.2), short], axis=0))
    now, base, sums = pl.pallas_call(
        first_kernel,
        in_specs=[VMEM] * 2,
        out_specs=[VMEM] * 3,
        out_shape=[jax.ShapeDtypeStruct((rows, width), F32)] * 2 + [jax.ShapeDtypeStruct((8, width), F32)],
        scratch_shapes=[pltpu.VMEM((rows - 2 * H, padded), BF16)] * 2,
        compiler_params=params(28),
        cost_estimate=pl.CostEstimate(flops=6 * 10**9, bytes_accessed=3 * 10**7, transcendentals=0),
        name="first_blur",
    )(pattern, first_taps)

    edge, edge_base, send = pl.pallas_call(
        edge_kernel,
        in_specs=[VMEM] * 6,
        out_specs=[VMEM] * 3,
        out_shape=[jax.ShapeDtypeStruct((4 * H, width), F32)] * 2 + [jax.ShapeDtypeStruct((count, LANES), F32)],
        compiler_params=params(28),
        name="edge_blur",
    )(for_odd, for_even, from_odd, from_even, sums, first_taps)

    gathered = lax.all_to_all(send.reshape(count, 1, LANES), AXES, 0, 0, tiled=True).reshape(count, LANES)

    cols = np.arange(cells, dtype=np.float64)
    across = back_weight(cols[:, None] - cols[None, :], fog_sigma)
    mix = np.zeros((LANES, 3 * LANES))
    for half in range(2):
        mine = slice(half * cells, (half + 1) * cells)
        other = slice((1 - half) * cells, (2 - half) * cells)
        mix[mine, mine] = across
        where = LANES if half == 1 else 2 * LANES
        mix[mine, where + other.start : where + other.stop] = across
    strips = np.arange(count, dtype=np.float64)
    gap = 2.0 * (strips[None, :] - strips[:, None])
    down = np.concatenate([back_weight(gap + shift, fog_sigma) for shift in (0.0, 1.0, -1.0)], axis=1)
    constants = [jnp.asarray(m) for m in two_terms(mix) + two_terms(down)]

    big = jnp.asarray(row_taps(wide, 1.0))
    small = jnp.asarray(row_taps(rows % wide, 1.0))
    return pl.pallas_call(
        second_kernel,
        in_specs=[VMEM] * 13,
        out_specs=[HBM] * 2,
        out_shape=[jax.ShapeDtypeStruct((rows, width), F32)] * 2,
        scratch_shapes=[pltpu.VMEM((rows, width), F32)] * 2
        + [pltpu.VMEM((rows, padded), BF16)] * 2
        + [pltpu.VMEM((8, width), F32)]
        + [pltpu.VMEM((count, LANES), F32)] * 2
        + [pltpu.SemaphoreType.DMA((cells,))] * 2,
        compiler_params=params(36),
        cost_estimate=pl.CostEstimate(flops=8 * 10**9, bytes_accessed=3 * 10**7, transcendentals=0),
        name="second_blur",
    )(now, base, edge, edge_base, gathered, *constants, big, small, taps_high, taps_low)


def solution(mesh):
    return jax.shard_map(
        local,
        mesh=mesh,
        in_specs=(P(AXES, None),),
        out_specs=(P(AXES, None), P(AXES, None)),
        check_vma=False,
    )
```
